128 devices in a mesh: sec: 2 (over y_lo), dev: 64 (over y_hi, x, z, core).
Axes of the slice: x: 4, y: 4 (y_hi: 2, y_lo: 2; y = y_hi * 2 + y_lo), z: 4, core: 2. Of those that a mesh axis runs over, the one named last changes fastest.
Arguments:
- flow_state: float32 [5, 8, 4096, 512], P(None, None, ('sec', 'dev')), may hold values from -6 to 6
- diffusion: float32 [8, 4096, 512], P(None, ('sec', 'dev')), may hold values from 0.02 to 0.1
- wall_stress: float32 [2, 4096, 512], P(None, ('sec', 'dev')), may hold values from -3 to 3
- batch_counts: int32 [128, 192], P(('sec', 'dev')), may hold values from 1 to 4, 480 in all within a row
- batch_routes: int32 [24576, 1], P(('sec', 'dev')), may hold values from 0 to 127; in each aligned block of 192 rows (0 to 191, 192 to 383, ...) at most 2 rows name the same one
- wall_index: int32 [24576, 4], P(('sec', 'dev')), may hold values from 0 to 16383, as said below
- input_weight: bfloat16 [12, 2048], replicated, may hold values from -1.75 to 1.75
- middle_weight: bfloat16 [2048, 2048], P(('sec', 'dev')), may hold values from -0.125 to 0.125
- output_weight: bfloat16 [2, 2048], replicated, may hold values from -0.125 to 0.125
Outputs:
- new_field: float32 [5, 8, 4096, 512], P(None, None, ('sec', 'dev'))
- new_stress: float32 [2, 4096, 512], P(None, ('sec', 'dev'))
- batch_loss: float32 [128], P(('sec', 'dev'))
- grad_w_in: float32 [12, 2048], replicated
- grad_w_mid: float32 [2048, 2048], P(('sec', 'dev'))
The draws below stay inside these ranges and needn't reach their ends.
Inputs may be any that keep to these rules, and one draw needn't show every extreme that they name: `batch_routes`: within the 192 rows of one device no trainer is named more than 2 times, and every trainer is named by some row. `batch_counts`: each device's row sums to 480. `wall_index`: all entries of the 192 rows of one device are distinct.
All inputs are finite; a program needn't handle non-finite values.
Results may differ from the reference program's by a relative error of at most 0.00091.
Values may be sent and summed in bfloat16 or wider, within the bound.
A program may use at most 128 MiB of HBM per device.

```python
import math
import jax
import jax.numpy as jnp
import numpy as np
from jax import lax

NV = 5
NL = 8
NX = 512
ZL = 32
CAP = 4
FEAT = 12
H = 2048
SLOTS = 2
NZ = 4096
TILES_DEV = 192
LIVE_DEV = 480
BATCHES = 24576
SAMPLES = 61440
DEVICES = 128


def draw_wall_index(key, part):
    points = ZL * NX
    owners = BATCHES // TILES_DEV
    keys = jax.random.split(key, owners)

    def one_owner(owner_key):
        order = jax.random.permutation(owner_key, points)
        chosen = order[:TILES_DEV * CAP]
        has_top = jnp.any(chosen == points - 1)
        chosen = chosen.at[0].set(jnp.where(has_top, chosen[0], points - 1))
        return chosen.reshape(TILES_DEV, CAP)
    return jax.vmap(one_owner)(keys).reshape(BATCHES, CAP).astype(jnp.int32)


def block_scale(rng, extent, cuts, smallest, top_value):
    def one(axis_at, parts):
        draws = jax.random.uniform(jax.random.fold_in(jax.random.fold_in(rng, 6), axis_at), (parts,), jnp.float32, smallest / len(cuts), top_value / len(cuts))
        return jnp.repeat(jnp.exp(draws), extent[axis_at] // parts).reshape((-1,) + (1,) * (len(extent) - axis_at - 1))

    level = one(*cuts[0])
    for cut in cuts[1:]:
        level = level * one(*cut)
    return level


def profile(count, total, bound, lean):
    portions = [(1 << 20) // math.isqrt(rank ** lean) + 1 for rank in range(2, count + 1)]
    spare, given = total - bound - (count - 1), [1] * (count - 1)
    while spare > 0:
        movable = [i for i in range(count - 1) if given[i] < bound]
        pool, remaining = sum([portions[i] for i in movable]), spare
        for i in movable:
            more = min(bound - given[i], max(1, remaining * portions[i] // pool), spare)
            given[i] = given[i] + more
            spare = spare - more
    return np.array([bound] + given)


def uneven(rng, count, total, limit, skew):
    if count == 2:
        one = jax.random.randint(rng, (), max(1, total - limit), min(limit, total - 1) + 1)
        return jnp.stack([one, total - one])
    tallies = jnp.asarray(profile(count, total, limit, skew), jnp.int32)
    pairs = (count - 1) // 2
    donor, taker = tallies[1:1 + 2 * pairs:2], tallies[2:2 + 2 * pairs:2]
    room = jnp.minimum(donor - 1, limit - taker)
    moved = jax.random.randint(jax.random.fold_in(rng, 1), (pairs,), 0, 1 << 20) % (room + 1)
    tallies = tallies.at[1:1 + 2 * pairs:2].set(donor - moved).at[2:2 + 2 * pairs:2].set(taker + moved)
    return tallies[jax.random.permutation(jax.random.fold_in(rng, 2), count)]


def assign_block(own_key, own, number, rows, amount, top, limit, lean):
    sequence = jax.random.permutation(own_key, amount)
    crowded, usual = load_shares(amount, rows * top, limit, lean, True), load_shares(amount, rows * top, limit, lean, False)
    places = jnp.arange(amount)

    def named(tallies, rotation):
        used = int((tallies > 0).sum())
        fixed = max(1, used // 4)
        shifted = fixed + (places - fixed + rotation * (used - fixed)) % max(1, amount - fixed)
        return jnp.zeros((amount,), jnp.int32).at[sequence[jnp.where(places < fixed, places, shifted)]].set(jnp.asarray(tallies, jnp.int32))

    tallies = jnp.where(number % 4 == 0, named(crowded, number // 4), named(usual, number - number // 4 - 1))
    mixed = jax.random.permutation(jax.random.fold_in(own, 3), amount)
    source_of, taker = mixed[0:amount // 2 * 2:2], mixed[1:amount // 2 * 2:2]
    room = jnp.minimum(tallies[source_of] - 1, limit - tallies[taker]) // 2
    room = jnp.where((source_of == sequence[0]) | (taker == sequence[0]) | (tallies[taker] == 0), 0, jnp.maximum(room, 0))
    shifted = jax.random.randint(jax.random.fold_in(own, 4), (amount // 2,), 0, 1 << 20) % (room + 1)
    tallies = tallies.at[source_of].add(-shifted).at[taker].add(shifted)
    labels = jnp.searchsorted(jnp.cumsum(tallies), jnp.arange(rows * top), side="right").astype(jnp.int32)
    listing = labels.reshape(top, rows).T
    listing = listing[jax.random.permutation(jax.random.fold_in(own, 1), rows)]
    rotation = jax.random.randint(jax.random.fold_in(own, 2), (rows, 1), 0, top)
    return jnp.take_along_axis(listing, (jnp.arange(top)[None, :] + rotation) % top, axis=1)


def load_shares(number_of, total, bound, slope, full):
    weights = [(1 << 20) // math.isqrt(grade ** slope) + 1 for grade in range(1, number_of + 1)]
    largest = bound if full else min(bound, max(-(-total // number_of), total * weights[0] // sum(weights)))
    least = 1 if total - largest >= number_of - 1 else 0
    given, surplus = [largest] + [least] * (number_of - 1), total - largest - least * (number_of - 1)
    while surplus > 0:
        movable = [i for i in range(1, number_of) if given[i] < largest] or [i for i in range(1, number_of) if given[i] < bound]
        pool, remaining = sum([weights[i] for i in movable]), surplus
        for i in movable:
            more = min(bound - given[i], max(1, remaining * weights[i] // pool), surplus)
            given[i] = given[i] + more
            surplus = surplus - more
    return np.array(given)


def scatter_about(rng, shape, width, limit, cuts=(), kind=jnp.bfloat16):
    gain = block_scale(rng, shape, cuts, -0.22, 0.18) if cuts else 1.0
    drawn = jax.random.normal(rng, shape, jnp.float32) * width * gain
    return jnp.minimum(jnp.maximum(drawn, -limit), limit).astype(kind)


def setup_inputs(seed: int = 0) -> dict:
    arg_keys = jax.random.split(jax.random.key(seed), 10)
    flow_state = scatter_about(arg_keys[0], (NV, NL, NZ, NX), 1.0, 6.0, ((2, 128),), jnp.float32)
    diffusion = jnp.clip(jnp.exp(math.log(0.1) - 1.609438 * jax.random.uniform(arg_keys[1], (NL, NZ, NX), jnp.float32) ** block_scale(arg_keys[1], (NL, NZ, NX), ((1, 128),), -0.2, 0.2)), 0.02, 0.1)
    wall_stress = scatter_about(arg_keys[2], (2, NZ, NX), 0.5, 3.0, ((1, 128),), jnp.float32)
    batch_counts = jax.vmap(lambda own: uneven(own, TILES_DEV, LIVE_DEV, CAP, 2))(jax.random.split(arg_keys[3], DEVICES)).reshape((DEVICES, TILES_DEV)).astype(jnp.int32)
    batch_routes_keys = jax.random.split(jax.random.fold_in(arg_keys[4], 1), BATCHES // TILES_DEV)
    batch_routes_turns = jax.random.permutation(jax.random.fold_in(arg_keys[4], 3), BATCHES // TILES_DEV)
    batch_routes = jax.vmap(lambda own, number: assign_block(jax.random.fold_in(arg_keys[4], 2), own, number, TILES_DEV, DEVICES, 1, SLOTS, 2))(batch_routes_keys, batch_routes_turns).reshape((BATCHES, 1))
    wall_index = draw_wall_index(jax.random.fold_in(arg_keys[9], 71), 0)
    input_weight = scatter_about(arg_keys[6], (FEAT, H), FEAT ** -0.5, 1.75)
    middle_weight = scatter_about(arg_keys[7], (H, H), H ** -0.5, 0.125, ((0, 128),))
    output_weight = scatter_about(arg_keys[8], (2, H), H ** -0.5, 0.125)
    return dict(flow_state=flow_state, diffusion=diffusion, wall_stress=wall_stress, batch_counts=batch_counts, batch_routes=batch_routes, wall_index=wall_index, input_weight=input_weight, middle_weight=middle_weight, output_weight=output_weight)


advect_number = 0.3
wall_gain = 0.5
grad_number = 32.0

def advance(flow_state, diffusion, below_z, above_z):
    below_x = jnp.concatenate([flow_state[..., :1], flow_state[..., :-1]], axis=3)
    above_x = jnp.concatenate([flow_state[..., 1:], flow_state[..., -1:]], axis=3)
    below_y = jnp.concatenate([flow_state[:, :1], flow_state[:, :-1]], axis=1)
    above_y = jnp.concatenate([flow_state[:, 1:], flow_state[:, -1:]], axis=1)
    spread = below_x + above_x + below_y + above_y + below_z + above_z - 6.0 * flow_state
    return flow_state + advect_number * (below_x - flow_state) + diffusion[None] * spread

def wall_columns(flow_state):
    points = flow_state.shape[2] * flow_state.shape[3]
    inputs = flow_state[0:4, 0:3].reshape(12, points)
    targets = jnp.stack([flow_state[1, 4] - flow_state[1, 3], flow_state[3, 4] - flow_state[3, 3]]).reshape(2, points)
    return jnp.concatenate([inputs, targets], axis=0).astype(jnp.bfloat16)

def apply_wall(advanced, new_stress):
    advanced = advanced.at[1, 0].add(-wall_gain * new_stress[0])
    return advanced.at[3, 0].add(-wall_gain * new_stress[1])

def reference(flow_state, diffusion, wall_stress, batch_counts, batch_routes, wall_index, input_weight, middle_weight, output_weight):
    owners, tile_count = batch_counts.shape
    batches, capacity = wall_index.shape
    points = ZL * NX
    owner_of = jnp.arange(batches, dtype=jnp.int32) // tile_count
    is_live = jnp.arange(capacity, dtype=jnp.int32)[None, :] < batch_counts.reshape(batches)[:, None]
    global_point = (wall_index + (owner_of * points)[:, None]).astype(jnp.int32)
    columns = wall_columns(flow_state)
    samples = jnp.take(columns, global_point.reshape(-1), axis=1)
    block_rows = tile_count * capacity
    sample_blocks = jnp.transpose(samples.reshape(14, owners, block_rows), (1, 0, 2))
    live_blocks = is_live.reshape(owners, block_rows).astype(jnp.float32)
    scale = grad_number / math.sqrt(SAMPLES)

    def step(carry, block):
        grad_in, grad_mid = carry
        rows, live_rows = block
        features = rows[:12].T
        targets = rows[12:].T.astype(jnp.float32)
        pre_first = jnp.dot(features, input_weight, preferred_element_type=jnp.float32)
        first_tanh = jnp.tanh(pre_first)
        first_act = first_tanh.astype(jnp.bfloat16)
        pre_second = jnp.dot(first_act, middle_weight, preferred_element_type=jnp.float32)
        second_tanh = jnp.tanh(pre_second)
        second_act = second_tanh.astype(jnp.bfloat16)
        prediction = jnp.dot(second_act, output_weight.T, preferred_element_type=jnp.float32)
        errors = (prediction - targets) * live_rows[:, None]
        back_out = (errors * scale).astype(jnp.bfloat16)
        back_second = (jnp.dot(back_out, output_weight, preferred_element_type=jnp.float32) * (1.0 - second_tanh * second_tanh)).astype(jnp.bfloat16)
        grad_mid = grad_mid + jnp.dot(first_act.T, back_second, preferred_element_type=jnp.float32)
        back_hidden = jnp.dot(back_second, middle_weight.T, preferred_element_type=jnp.float32)
        back_first = (back_hidden * (1.0 - first_tanh * first_tanh)).astype(jnp.bfloat16)
        grad_in = grad_in + jnp.dot(features.T, back_first, preferred_element_type=jnp.float32)
        return ((grad_in, grad_mid), (prediction.astype(jnp.bfloat16), lax.optimization_barrier(jnp.sum(errors * errors, axis=1))))
    init = (jnp.zeros((12, H), jnp.float32), jnp.zeros((H, H), jnp.float32))
    (grad_w_in, grad_w_mid), (sent, squares) = lax.scan(step, init, (sample_blocks, live_blocks))
    sent = sent.reshape(batches * capacity, 2)
    batch_sq = lax.optimization_barrier(jnp.sum(squares.reshape(batches, capacity), axis=1))
    route_flat = batch_routes.reshape(batches)
    matches = route_flat[:, None] == jnp.arange(owners, dtype=jnp.int32)[None, :]
    loss_sum = lax.optimization_barrier(jnp.sum(jnp.where(matches, batch_sq[:, None], jnp.zeros((), jnp.float32)), axis=0))
    count_float = batch_counts.reshape(batches).astype(jnp.float32)
    live_count = lax.optimization_barrier(jnp.sum(jnp.where(matches, count_float[:, None], jnp.zeros((), jnp.float32)), axis=0))
    batch_loss = 0.5 * loss_sum / live_count
    total_points = wall_stress.shape[1] * wall_stress.shape[2]
    target_index = jnp.where(is_live, global_point, total_points).reshape(-1)
    new_stress = wall_stress.reshape(2, total_points).at[:, target_index].set(sent.astype(jnp.float32).T, mode='drop').reshape(wall_stress.shape)
    below_z = jnp.roll(flow_state, 1, axis=2)
    above_z = jnp.roll(flow_state, -1, axis=2)
    advanced = advance(flow_state, diffusion, below_z, above_z)
    new_field = apply_wall(advanced, new_stress)
    return (new_field, new_stress, batch_loss, grad_w_in, grad_w_mid)
```

```python
import math

import jax
import jax.numpy as jnp
from jax import lax
from jax.experimental import pallas as pl
from jax.experimental.pallas import tpu as pltpu
from jax.sharding import PartitionSpec as P

BF = jnp.bfloat16
F32 = jnp.float32
MESH = pl.DeviceIdType.MESH

H = 2048
CAP = 4
TILES = 192
LIVE = 480
PAD = 512
GROUP = 8
COLS = H // GROUP
S = GROUP * LIVE
CH = 1280
NCH = S // CH
JT = 512
DEVICES = 128
ADVECT = 0.3
GAIN = 0.5
SCALE = 32.0 / math.sqrt(LIVE * DEVICES)


def nn(a, b):
    return jnp.dot(a, b, preferred_element_type=F32)


def nt(a, b):
    return lax.dot_general(a, b, (((1,), (1,)), ((), ())), preferred_element_type=F32)


def tn(a, b):
    return lax.dot_general(a, b, (((0,), (0,)), ((), ())), preferred_element_type=F32)


def iota(shape, dim):
    return lax.broadcasted_iota(jnp.int32, shape, dim)


def train_kernel(
    flow, counts, routes, index, win, wmid, wout,
    halo_out, meta_out, small_out, gmid_out,
    t, fs, w, wct, d2, bst, gm, ra, rb, acc_a, acc_b, r2a, r2b, fin,
    planes, tplanes, edge, wsrc, wint, wpad, own, fbuf, ftot, feats, pbuf, rowmeta, perr,
    gwp, rg, rgx, rgy,
    lsem, ssem, rsem,
):
    sec = lax.axis_index("sec")
    dev = lax.axis_index("dev")
    m = dev % 8
    x = (dev // 8) % 4
    yh = dev // 32
    y = yh * 2 + sec
    yq = sec * 2 + yh
    flat = sec * 64 + dev
    used = [0]

    def send(src, dst, to):
        i = used[0]
        used[0] += 1
        copy = pltpu.make_async_remote_copy(
            src_ref=src, dst_ref=dst, send_sem=ssem.at[i], recv_sem=rsem.at[i],
            device_id=to, device_id_type=MESH,
        )
        copy.start()
        return copy

    members = [((m + k) % 8, (sec, dev - m + (m + k) % 8)) for k in range(1, 8)]
    xs = [((x + k) % 4, (sec, yh * 32 + ((x + k) % 4) * 8 + m)) for k in (1, 3, 2)]
    ys = []
    for k in (1, 3, 2):
        yy = (y + k) % 4
        ys.append(((yy % 2) * 2 + yy // 2, (yy % 2, (yy // 2) * 32 + x * 8 + m)))
    up = (flat + 1) % 128
    down = (flat + 127) % 128
    up_id = (up // 64, up % 64)
    down_id = (down // 64, down % 64)

    loads = [
        pltpu.make_async_copy(flow.at[0:4, 0:3], planes, lsem.at[0]),
        pltpu.make_async_copy(flow.at[1, 3:5], tplanes.at[0], lsem.at[1]),
        pltpu.make_async_copy(flow.at[3, 3:5], tplanes.at[1], lsem.at[2]),
        pltpu.make_async_copy(flow.at[:, :, 0:8, :], edge.at[0], lsem.at[3]),
        pltpu.make_async_copy(flow.at[:, :, 24:32, :], edge.at[1], lsem.at[4]),
    ]
    for copy in loads:
        copy.start()

    barrier = pltpu.get_barrier_semaphore()
    partners = [p for _, p in members] + [p for _, p in xs] + [p for _, p in ys] + [up_id, down_id]
    for p in partners:
        pl.semaphore_signal(barrier, inc=1, device_id=p, device_id_type=MESH)

    for i in range(GROUP):
        for h in range(2):
            wsrc[i, h] = wmid[:, COLS * i + 128 * h:COLS * i + 128 * h + 128]
    winp = jnp.concatenate([win[...].astype(F32), jnp.zeros((4, H), F32)], axis=0)
    wint[...] = winp.T.astype(BF)
    wpad[...] = jnp.zeros_like(wpad)
    wpad[0:2, :] = wout[:, pl.ds(pl.multiple_of(m * COLS, COLS), COLS)].astype(F32)

    pl.semaphore_wait(barrier, len(partners))

    mine = pl.ds(pl.multiple_of(m * 16, 16), 16)
    w0 = [send(wsrc.at[mm], w.at[:, yq, x, mine, :], to) for mm, to in members]
    w[:, yq, x, mine, :] = wsrc[m]

    for copy in loads:
        copy.wait()
    halo_src = own
    halo_src[0] = edge[0, :, :, 0, :]
    halo_src[1] = edge[1, :, :, 7, :]
    halos = [
        send(halo_src.at[0], halo_out.at[1], down_id),
        send(halo_src.at[1], halo_out.at[0], up_id),
    ]

    cnt = jnp.broadcast_to(counts[...].astype(F32), (16, TILES)).astype(BF)
    r_i, c_i = iota((TILES, TILES), 0), iota((TILES, TILES), 1)
    start = nt((c_i < r_i).astype(F32).astype(BF), cnt)[:, 0:1]
    ends = nt((c_i <= r_i).astype(F32).astype(BF), cnt)[:, 0:1]
    place = iota((TILES, PAD), 1).astype(F32)
    onehot = jnp.where((place >= start) & (place < ends), 1.0, 0.0).astype(BF)
    idx = index[...]
    lane16 = iota((TILES, 16), 1)
    table = jnp.zeros((TILES, 16), jnp.int32)
    start_i = start.astype(jnp.int32)
    pieces = []
    for k in range(CAP):
        col = idx[:, k:k + 1]
        pieces += [(k, col >> 9), (4 + k, (col >> 4) & 31), (8 + k, col & 15)]
    pieces += [(12, start_i >> 4), (13, start_i & 15), (14, routes[...])]
    for at, col in pieces:
        table = jnp.where(lane16 == at, col, table)
    vals = tn(table.astype(F32).astype(BF), onehot)
    lane = iota((1, PAD), 1)
    kk = lane.astype(F32) - (vals[12:13] * 16.0 + vals[13:14])
    zrow = jnp.zeros((1, PAD), F32)
    xrow = jnp.zeros((1, PAD), F32)
    for k in range(CAP):
        hit = kk == float(k)
        zrow = jnp.where(hit, vals[k:k + 1], zrow)
        xrow = jnp.where(hit, vals[4 + k:5 + k] * 16.0 + vals[8 + k:9 + k], xrow)
    valid = lane < LIVE
    zrow = jnp.where(valid, zrow, -1.0)
    xrow = jnp.where(valid, xrow, -1.0)
    rowmeta[0:1, :] = zrow
    rowmeta[1:2, :] = xrow
    rowmeta[2:3, :] = jnp.where(valid, vals[14:15], -1.0)
    oz = jnp.where(iota((32, PAD), 0).astype(F32) == zrow, 1.0, 0.0)
    ox = jnp.where(iota((PAD, PAD), 0).astype(F32) == xrow, 1.0, 0.0).astype(BF)
    tp = jnp.stack([tplanes[0, 1] - tplanes[0, 0], tplanes[1, 1] - tplanes[1, 0]])
    table_p = jnp.concatenate(
        [planes[...].reshape(384, PAD).astype(BF), tp.reshape(64, PAD).astype(BF)], axis=0
    )
    got = nn(table_p, ox).reshape(14, 32, PAD) * oz[None]
    picked = jnp.sum(got, axis=1)
    picked = jnp.concatenate([picked, jnp.zeros((2, PAD), F32)], axis=0)
    fbuf[m] = picked.astype(BF)
    fcopies = [send(fbuf.at[m], fbuf.at[m], to) for _, to in members]

    for copy in w0:
        copy.wait()
    w1 = [send(w.at[0, yq, x], w.at[0, yq, x], to) for _, to in xs]
    w1 += [send(w.at[1, yq, x], w.at[1, yq, x], to) for _, to in ys]

    for copy in fcopies:
        copy.wait()
    ftot[...] = jnp.zeros_like(ftot)
    for i in range(GROUP):
        base, rest = divmod(LIVE * i, 128)
        wide = jnp.concatenate([fbuf[i].astype(F32), jnp.zeros((16, 128), F32)], axis=1)
        if rest:
            wide = pltpu.roll(wide, rest, 1)
        ftot[:, 128 * base:128 * base + PAD + 128] += wide
    feats[...] = ftot[:, 0:S].astype(BF)

    for copy in w1:
        copy.wait()
    w2 = [send(w.at[0, yq], w.at[0, yq], to) for _, to in ys]
    w2 += [send(w.at[1, :, x], w.at[1, :, x], to) for _, to in xs]

    def first(q):
        sl = slice(CH * q, CH * q + CH)

        def inner(j, _):
            rows = pl.ds(pl.multiple_of(j * JT, JT), JT)
            act = jnp.tanh(nn(wint[rows, :], feats[:, sl]))
            t[rows, sl] = act
            fs[rows, :] = act.astype(BF)
            return 0

        lax.fori_loop(0, H // JT, inner, 0, unroll=True)

    for q in range(NCH):
        sl = slice(CH * q, CH * q + CH)
        first(q)
        if q == 0:
            for copy in w2:
                copy.wait()
            for h in range(2):
                wct[128 * h:128 * h + 128, :] = w[h].reshape(H, 128).astype(F32).T.astype(BF)
        act2 = jnp.tanh(nn(wct[...], fs[...]))
        d2[:, sl] = 1.0 - act2 * act2
        pbuf[m, 2 * q:2 * q + 2, :] = nn(wpad[...].astype(BF), act2.astype(BF))[0:2]
    pbuf[m, 6:8, :] = jnp.zeros((2, CH), F32)
    pcopies = [send(pbuf.at[m], pbuf.at[m], to) for _, to in members]
    for copy in pcopies:
        copy.wait()

    total = pbuf[0]
    for i in range(1, GROUP):
        total = total + pbuf[i]
    pred = jnp.concatenate([total[2 * q:2 * q + 2] for q in range(NCH)], axis=1)
    err = pred - ftot[12:14, 0:S]
    perr[0:2, :] = pred
    perr[2:4, :] = err
    perr[4:8, :] = jnp.zeros((4, S), F32)
    bo = (perr[...] * SCALE)
    bo = jnp.concatenate([bo[2:4], jnp.zeros((14, S), F32)], axis=0).astype(BF)
    for q in range(NCH):
        sl = slice(CH * q, CH * q + CH)
        bst[:, sl] = (tn(wpad[...].astype(BF), bo[:, sl]) * d2[:, sl]).astype(BF)

    def mid(q, _):
        rows = pl.ds(pl.multiple_of(q * JT, JT), JT)
        part = nt(t[rows, :].astype(BF), bst[...])
        for h in range(2):
            gm[h, q] = part[:, 128 * h:128 * h + 128].reshape(4, 128, 128)
        return 0

    lax.fori_loop(0, H // JT, mid, 0)
    s1 = [send(gm.at[0, :, xx], ra.at[i], to) for i, (xx, to) in enumerate(xs)]
    s1 += [send(gm.at[1, yy], rb.at[i], to) for i, (yy, to) in enumerate(ys)]

    rolled = pltpu.roll(perr[...], (S - LIVE * m) % S, 1)[:, 0:PAD]
    meta_out[0:2, :] = jnp.where(valid, rolled[0:2], 0.0)
    meta_out[2:4, :] = rowmeta[0:2, :]
    meta_out[4:8, :] = jnp.zeros((4, PAD), F32)
    square = rolled[2:3] * rolled[2:3] + rolled[3:4] * rolled[3:4]
    square = jnp.where(valid, square, 0.0)
    chosen = iota((DEVICES, PAD), 0).astype(F32) == rowmeta[2:3, :]
    loss_col = jnp.sum(jnp.where(chosen, square, 0.0), axis=1, keepdims=True)
    count_col = jnp.sum(jnp.where(chosen, 1.0, 0.0), axis=1, keepdims=True)
    loss_row = jnp.broadcast_to(loss_col, (DEVICES, DEVICES)).T[0:1]
    count_row = jnp.broadcast_to(count_col, (DEVICES, DEVICES)).T[0:1]

    def back(q, _):
        rows = pl.ds(pl.multiple_of(q * JT, JT), JT)
        wc = jnp.concatenate([w[0, q].reshape(JT, 128), w[1, q].reshape(JT, 128)], axis=1)
        acc = jnp.zeros((16, JT), F32)
        for s in range(NCH):
            sl = slice(CH * s, CH * s + CH)
            act = t[rows, sl]
            bf = (nn(wc, bst[:, sl]) * (1.0 - act * act)).astype(BF)
            acc = acc + nt(feats[:, sl], bf)
        gwp[:, rows] = acc
        return 0

    lax.fori_loop(0, H // JT, back, 0)
    gwp[12:16, :] = jnp.zeros((4, H), F32)
    gwp[12:13, 0:DEVICES] = loss_row
    gwp[13:14, 0:DEVICES] = count_row

    g1 = [
        send(gwp.at[:, pl.ds(pl.multiple_of(mm * COLS, COLS), COLS)], rg.at[i], to)
        for i, (mm, to) in enumerate(members)
    ]
    for copy in s1:
        copy.wait()
    acc_a[...] = gm[0, :, x] + ra[0] + ra[1] + ra[2]
    acc_b[...] = gm[1, yq] + rb[0] + rb[1] + rb[2]
    s2 = [send(acc_a.at[yy], r2a.at[i], to) for i, (yy, to) in enumerate(ys)]
    s2 += [send(acc_b.at[xx], r2b.at[i], to) for i, (xx, to) in enumerate(xs)]

    my_cols = pl.ds(pl.multiple_of(m * COLS, COLS), COLS)
    for copy in g1:
        copy.wait()
    part = gwp[:, my_cols]
    for i in range(7):
        part = part + rg[i]
    rgx[x] = part
    g2 = [send(rgx.at[x], rgx.at[x], to) for _, to in xs]
    for copy in g2:
        copy.wait()
    rgy[yq] = (rgx[0] + rgx[1]) + (rgx[2] + rgx[3])
    g3 = [send(rgy.at[yq], rgy.at[yq], to) for _, to in ys]

    for copy in s2:
        copy.wait()
    fin[0] = acc_a[yq] + r2a[0] + r2a[1] + r2a[2]
    fin[1] = acc_b[x] + r2b[0] + r2b[1] + r2b[2]
    s3 = [
        send(fin.at[:, pl.ds(pl.multiple_of(mm * 16, 16), 16), :], gmid_out.at[m], to)
        for mm, to in members
    ]
    gmid_out[m] = fin[:, mine, :]

    for copy in g3:
        copy.wait()
    small_out[m] = (rgy[0] + rgy[1]) + (rgy[2] + rgy[3])
    g4 = [send(small_out.at[m], small_out.at[m], to) for _, to in members]
    for copy in s3 + g4 + halos:
        copy.wait()


N_SENDS = 7 + 2 + 7 + 6 + 6 + 7 + 6 + 7 + 6 + 3 + 3 + 7 + 7


def train(flow, counts, routes, index, win, wmid, wout):
    vm = pl.BlockSpec(memory_space=pltpu.VMEM)
    sds = jax.ShapeDtypeStruct
    return pl.pallas_call(
        train_kernel,
        out_shape=(
            sds((2, 5, 8, 512), F32),
            sds((8, PAD), F32),
            sds((GROUP, 16, COLS), F32),
            sds((GROUP, 2, 16, 128), F32),
        ),
        in_specs=[pl.BlockSpec(memory_space=pl.ANY)] + [vm] * 6,
        out_specs=(vm,) * 4,
        scratch_shapes=[
            pltpu.VMEM((H, S), F32),
            pltpu.VMEM((H, CH), BF),
            pltpu.VMEM((2, 4, 4, 128, 128), BF),
            pltpu.VMEM((COLS, H), BF),
            pltpu.VMEM((COLS, S), F32),
            pltpu.VMEM((COLS, S), BF),
            pltpu.VMEM((2, 4, 4, 128, 128), F32),
            pltpu.VMEM((3, 4, 128, 128), F32),
            pltpu.VMEM((3, 4, 128, 128), F32),
            pltpu.VMEM((4, 128, 128), F32),
            pltpu.VMEM((4, 128, 128), F32),
            pltpu.VMEM((3, 128, 128), F32),
            pltpu.VMEM((3, 128, 128), F32),
            pltpu.VMEM((2, 128, 128), F32),
            pltpu.VMEM((4, 3, 32, 512), F32),
            pltpu.VMEM((2, 2, 32, 512), F32),
            pltpu.VMEM((2, 5, 8, 8, 512), F32),
            pltpu.VMEM((GROUP, 2, 16, 128), BF),
            pltpu.VMEM((H, 16), BF),
            pltpu.VMEM((16, COLS), F32),
            pltpu.VMEM((2, 5, 8, 512), F32),
            pltpu.VMEM((GROUP, 16, PAD), BF),
            pltpu.VMEM((16, S + 128), F32),
            pltpu.VMEM((16, S), BF),
            pltpu.VMEM((GROUP, 8, CH), F32),
            pltpu.VMEM((8, PAD), F32),
            pltpu.VMEM((8, S), F32),
            pltpu.VMEM((16, H), F32),
            pltpu.VMEM((7, 16, COLS), F32),
            pltpu.VMEM((4, 16, COLS), F32),
            pltpu.VMEM((4, 16, COLS), F32),
            pltpu.SemaphoreType.DMA((5,)),
            pltpu.SemaphoreType.DMA((N_SENDS,)),
            pltpu.SemaphoreType.DMA((N_SENDS,)),
        ],
        compiler_params=pltpu.CompilerParams(
            collective_id=0, has_side_effects=True, vmem_limit_bytes=62 * 2**20
        ),
        name="train",
    )(flow, counts, routes, index, win, wmid, wout)


def slab_kernel(flow, diff, stress, halo, meta, small, gmid, field, new_stress, loss, gw, gwm):
    v = pl.program_id(0)

    @pl.when(v == 0)
    def _():
        zrow, xrow = meta[2:3, :], meta[3:4, :]
        oz = jnp.where(iota((32, PAD), 0).astype(F32) == zrow, 1.0, 0.0)
        ox = jnp.where(iota((PAD, PAD), 0).astype(F32) == xrow, 1.0, 0.0).astype(BF)
        lhs = jnp.concatenate([oz * meta[0:1, :], oz * meta[1:2, :], oz], axis=0).astype(BF)
        spread = nt(lhs, ox)
        hit = spread[64:96] > 0.5
        new_stress[0] = jnp.where(hit, spread[0:32], stress[0])
        new_stress[1] = jnp.where(hit, spread[32:64], stress[1])
        me = lax.axis_index("sec") * 64 + lax.axis_index("dev")
        ratio = 0.5 * small[0, 12:13, 0:DEVICES] / small[0, 13:14, 0:DEVICES]
        loss[0] = jnp.sum(jnp.where(iota((1, DEVICES), 1) == me, ratio, 0.0))
        for i in range(GROUP):
            gw[:, COLS * i:COLS * i + COLS] = small[i, 0:12, :]
            for h in range(2):
                at = COLS * i + 128 * h
                gwm[:, at:at + 128] = gmid[i, h]

    u = flow[0]
    row, col = iota((8, 32, 512), 1), iota((8, 32, 512), 2)
    below_z = jnp.where(row == 0, halo[0, v][:, None, :], pltpu.roll(u, 1, 1))
    above_z = jnp.where(row == 31, halo[1, v][:, None, :], pltpu.roll(u, 31, 1))
    below_x = jnp.where(col == 0, u, pltpu.roll(u, 1, 2))
    above_x = jnp.where(col == 511, u, pltpu.roll(u, 511, 2))
    below_y = jnp.concatenate([u[0:1], u[0:7]], axis=0)
    above_y = jnp.concatenate([u[1:8], u[7:8]], axis=0)
    spread = below_x + above_x + below_y + above_y + below_z + above_z - 6.0 * u
    field[0] = u + ADVECT * (below_x - u) + diff[...] * spread

    @pl.when(v == 1)
    def _():
        field[0, 0] = field[0, 0] - GAIN * new_stress[0]

    @pl.when(v == 3)
    def _():
        field[0, 0] = field[0, 0] - GAIN * new_stress[1]


def slab(flow, diff, stress, halo, meta, small, gmid):
    sds = jax.ShapeDtypeStruct

    def whole(shape):
        return pl.BlockSpec(shape, lambda v: (0,) * len(shape))

    block = pl.BlockSpec((1, 8, 32, 512), lambda v: (v, 0, 0, 0))
    return pl.pallas_call(
        slab_kernel,
        grid=(5,),
        out_shape=(
            sds((5, 8, 32, 512), F32),
            sds((2, 32, 512), F32),
            sds((1,), F32),
            sds((12, H), F32),
            sds((16, H), F32),
        ),
        in_specs=[
            block, whole((8, 32, 512)), whole((2, 32, 512)), whole((2, 5, 8, 512)),
            whole((8, PAD)), whole((GROUP, 16, COLS)), whole((GROUP, 2, 16, 128)),
        ],
        out_specs=(
            block, whole((2, 32, 512)), pl.BlockSpec(memory_space=pltpu.SMEM),
            whole((12, H)), whole((16, H)),
        ),
        compiler_params=pltpu.CompilerParams(vmem_limit_bytes=32 * 2**20),
        name="slab",
    )(flow, diff, stress, halo, meta, small, gmid)


def body(flow, diff, stress, counts, routes, index, win, wmid, wout):
    halo, meta, small, gmid = train(flow, counts, routes, index, win, wmid, wout)
    return slab(flow, diff, stress, halo, meta, small, gmid)


def solution(mesh):
    both = ("sec", "dev")
    in_specs = (
        P(None, None, both, None), P(None, both, None), P(None, both, None),
        P(both, None), P(both, None), P(both, None), P(), P(both, None), P(),
    )
    out_specs = (P(None, None, both, None), P(None, both, None), P(both), P(), P(both, None))
    return jax.shard_map(body, mesh=mesh, in_specs=in_specs, out_specs=out_specs, check_vma=False)
```

```python
import math

import jax
import jax.numpy as jnp
from jax import lax
from jax.experimental import pallas as pl
from jax.experimental.pallas import tpu as pltpu
from jax.sharding import PartitionSpec as P

BF = jnp.bfloat16
F32 = jnp.float32
MESH = pl.DeviceIdType.MESH

H = 2048
CAP = 4
TILES = 192
LIVE = 480
PAD = 512
GROUP = 8
COLS = H // GROUP
S = GROUP * LIVE
CH = 1280
NCH = S // CH
PARTS = ((0, 1280, 0), (1280, 640, 1280), (1920, 1280, 0), (3200, 640, 1280))
JT = 512
DEVICES = 128
ADVECT = 0.3
GAIN = 0.5
SCALE = 32.0 / math.sqrt(LIVE * DEVICES)


def nn(a, b):
    return jnp.dot(a, b, preferred_element_type=F32)


def nt(a, b):
    return lax.dot_general(a, b, (((1,), (1,)), ((), ())), preferred_element_type=F32)


def tn(a, b):
    return lax.dot_general(a, b, (((0,), (0,)), ((), ())), preferred_element_type=F32)


def iota(shape, dim):
    return lax.broadcasted_iota(jnp.int32, shape, dim)


def train_kernel(
    flow, counts_h, routes_h, index_h, win_h, wmid_h, wout_h,
    halo_out, meta_out, small_out, gmid_out,
    t, fs, w, wct, d2, bst, gm, ra, rb, r2a, r2b, fin,
    planes, tplanes, wsrc, wint, wpad, own, fbuf, ftot, feats, pbuf, rowmeta, perr,
    gwp, rg, rgp, counts, routes, index, win, wmid, wout, table,
    lsem, ssem, rsem,
):
    sec = lax.axis_index("sec")
    dev = lax.axis_index("dev")
    m = dev % 8
    x = (dev // 8) % 4
    yh = dev // 32
    y = yh * 2 + sec
    yq = sec * 2 + yh
    flat = sec * 64 + dev
    used = [0]

    def send(src, dst, to):
        i = used[0]
        used[0] += 1
        copy = pltpu.make_async_remote_copy(
            src_ref=src, dst_ref=dst, send_sem=ssem.at[i], recv_sem=rsem.at[i],
            device_id=to, device_id_type=MESH,
        )
        copy.start()
        return copy

    def at_plane(yy, xx):
        return (yy % 2, (yy // 2) * 32 + xx * 8 + m)

    members = [((m + k) % 8, (sec, dev - m + (m + k) % 8)) for k in range(1, 8)]
    xs = [((x + k) % 4, at_plane(y, (x + k) % 4)) for k in (1, 3, 2)]
    ys = []
    for k in (1, 3, 2):
        yy = (y + k) % 4
        ys.append(((yy % 2) * 2 + yy // 2, at_plane(yy, x)))
    plane = [
        at_plane((y + a) % 4, (x + b) % 4) for a in range(4) for b in range(4) if a or b
    ]
    up = (flat + 1) % 128
    down = (flat + 127) % 128
    up_id = (up // 64, up % 64)
    down_id = (down // 64, down % 64)

    barrier = pltpu.get_barrier_semaphore()
    partners = [p for _, p in members] + plane + [up_id, down_id]
    for p in partners:
        pl.semaphore_signal(barrier, inc=1, device_id=p, device_id_type=MESH)

    pairs = [
        (counts_h, counts), (routes_h, routes), (index_h, index), (win_h, win),
        (wout_h, wout), (wmid_h, wmid),
        (flow.at[0:4, 0:3], planes), (flow.at[1, 3:5], tplanes.at[0]),
        (flow.at[3, 3:5], tplanes.at[1]), (flow.at[:, :, 0, :], own.at[0]),
        (flow.at[:, :, 31, :], own.at[1]),
    ]
    loads = [pltpu.make_async_copy(a, b, lsem.at[i]) for i, (a, b) in enumerate(pairs)]
    for copy in loads:
        copy.start()
    for copy in loads[:6]:
        copy.wait()

    for i in range(GROUP):
        for h in range(2):
            wsrc[i, h] = wmid[:, COLS * i + 128 * h:COLS * i + 128 * h + 128]
    winp = jnp.concatenate([win[...].astype(F32), jnp.zeros((4, H), F32)], axis=0)
    wint[...] = winp.T.astype(BF)
    wpad[...] = jnp.zeros_like(wpad)
    wpad[0:2, :] = wout[:, pl.ds(pl.multiple_of(m * COLS, COLS), COLS)].astype(F32)

    cnt = jnp.broadcast_to(counts[...].astype(F32), (16, TILES)).astype(BF)
    r_i, c_i = iota((TILES, TILES), 0), iota((TILES, TILES), 1)
    start = nt((c_i < r_i).astype(F32).astype(BF), cnt)[:, 0:1]
    ends = nt((c_i <= r_i).astype(F32).astype(BF), cnt)[:, 0:1]
    start_row = nn(cnt, (r_i < c_i).astype(F32).astype(BF))[0:1].astype(jnp.int32)
    place = iota((TILES, PAD), 1).astype(F32)
    onehot = jnp.where((place >= start) & (place < ends), 1.0, 0.0).astype(BF)
    idx = index[...]
    table[...] = jnp.zeros_like(table)
    table[0:4, :] = (idx >> 9).astype(F32)
    table[4:8, :] = ((idx >> 4) & 31).astype(F32)
    table[8:12, :] = (idx & 15).astype(F32)
    table[12:13, :] = (start_row >> 4).astype(F32)
    table[13:14, :] = (start_row & 15).astype(F32)
    table[14:15, :] = routes[...].astype(F32)
    vals = nn(table[...].astype(BF), onehot)
    lane = iota((1, PAD), 1)
    kk = lane.astype(F32) - (vals[12:13] * 16.0 + vals[13:14])
    zrow = jnp.zeros((1, PAD), F32)
    xrow = jnp.zeros((1, PAD), F32)
    for k in range(CAP):
        hit = kk == float(k)
        zrow = jnp.where(hit, vals[k:k + 1], zrow)
        xrow = jnp.where(hit, vals[4 + k:5 + k] * 16.0 + vals[8 + k:9 + k], xrow)
    valid = lane < LIVE
    zrow = jnp.where(valid, zrow, -1.0)
    xrow = jnp.where(valid, xrow, -1.0)
    rowmeta[0:1, :] = zrow
    rowmeta[1:2, :] = xrow
    rowmeta[2:3, :] = jnp.where(valid, vals[14:15], -1.0)
    oz = jnp.where(iota((32, PAD), 0).astype(F32) == zrow, 1.0, 0.0)
    ox = jnp.where(iota((PAD, PAD), 0).astype(F32) == xrow, 1.0, 0.0).astype(BF)
    for copy in loads[6:]:
        copy.wait()
    tp = jnp.stack([tplanes[0, 1] - tplanes[0, 0], tplanes[1, 1] - tplanes[1, 0]])
    table_p = jnp.concatenate(
        [planes[...].reshape(384, PAD).astype(BF), tp.reshape(64, PAD).astype(BF)], axis=0
    )
    got = nn(table_p, ox).reshape(14, 32, PAD) * oz[None]
    picked = jnp.sum(got, axis=1)
    picked = jnp.concatenate([picked, jnp.zeros((2, PAD), F32)], axis=0)
    fbuf[m] = picked.astype(BF)

    pl.semaphore_wait(barrier, len(partners))

    mine = pl.ds(pl.multiple_of(m * 16, 16), 16)
    w0 = [send(wsrc.at[mm], w.at[:, yq, x, mine, :], to) for mm, to in members]
    w[:, yq, x, mine, :] = wsrc[m]
    fcopies = [send(fbuf.at[m], fbuf.at[m], to) for _, to in members]
    for copy in w0:
        copy.wait()
    w1x = [send(w.at[:, yq, x], w.at[:, yq, x], to) for _, to in xs]
    w1y = [send(w.at[:, yq, x], w.at[:, yq, x], to) for _, to in ys]
    for copy in fcopies:
        copy.wait()
    ftot[...] = jnp.zeros_like(ftot)
    for i in range(GROUP):
        base, rest = divmod(LIVE * i, 128)
        wide = jnp.concatenate([fbuf[i].astype(F32), jnp.zeros((16, 128), F32)], axis=1)
        if rest:
            wide = pltpu.roll(wide, rest, 1)
        ftot[:, 128 * base:128 * base + PAD + 128] += wide
    feats[...] = ftot[:, 0:S].astype(BF)

    w2 = []
    for i, k in enumerate((1, 3, 2)):
        w1x[i].wait()
        xx = (x + 4 - k) % 4
        w2 += [send(w.at[0, yq, xx], w.at[0, yq, xx], to) for _, to in ys]
        w1y[i].wait()
        yy = (y + 4 - k) % 4
        qq = (yy % 2) * 2 + yy // 2
        w2 += [send(w.at[1, qq, x], w.at[1, qq, x], to) for _, to in xs]
    halos = [
        send(own.at[0], halo_out.at[1], down_id),
        send(own.at[1], halo_out.at[0], up_id),
    ]

    def first(q):
        at, size, slot = PARTS[q]
        sl = slice(at, at + size)

        def inner(j, _):
            rows = pl.ds(pl.multiple_of(j * JT, JT), JT)
            act = jnp.tanh(nn(wint[rows, :], feats[:, sl]))
            t[rows, sl] = act
            fs[rows, slot:slot + size] = act.astype(BF)
            return 0

        lax.fori_loop(0, H // JT, inner, 0, unroll=True)

    pcopies = []

    def second(q):
        at, size, slot = PARTS[q]
        act2 = jnp.tanh(nn(wct[...], fs[:, slot:slot + size]))
        d2[:, at:at + size] = 1.0 - act2 * act2
        pbuf[m, q, :, 0:size] = nn(wpad[...].astype(BF), act2.astype(BF))[0:2]
        ref = pbuf.at[m, q, :, 0:size]
        pcopies.append([send(ref, ref, to) for _, to in members])

    first(0)
    first(1)
    for copy in w2:
        copy.wait()
    for h in range(2):
        wct[128 * h:128 * h + 128, :] = w[h].reshape(H, 128).astype(F32).T.astype(BF)
    second(0)
    first(2)
    second(1)
    first(3)
    second(2)
    second(3)
    perr[4:8, :] = jnp.zeros((4, S), F32)
    for q, (at, size, _) in enumerate(PARTS):
        sl = slice(at, at + size)
        for copy in pcopies[q]:
            copy.wait()
        pred = pbuf[0, q, :, 0:size]
        for i in range(1, GROUP):
            pred = pred + pbuf[i, q, :, 0:size]
        err = pred - ftot[12:14, sl]
        perr[0:2, sl] = pred
        perr[2:4, sl] = err
        bo = jnp.concatenate([err * SCALE, jnp.zeros((14, size), F32)], axis=0).astype(BF)
        bst[:, sl] = (tn(wpad[...].astype(BF), bo) * d2[:, sl]).astype(BF)

    s1a = []
    s1b = []
    for n, k in enumerate((1, 3, 2, 0)):
        yy = (y + k) % 4
        q = (yy % 2) * 2 + yy // 2
        rows = pl.ds(pl.multiple_of(q * JT, JT), JT)
        part = nt(t[rows, :].astype(BF), bst[...])
        for h in range(2):
            gm[h, q] = part[:, 128 * h:128 * h + 128].reshape(4, 128, 128)
        if k:
            s1b.append(send(gm.at[1, q], rb.at[n], ys[n][1]))
        for i, (xx, to) in enumerate(xs):
            s1a.append(send(gm.at[0, q, xx], ra.at[i, q], to))

    rolled = pltpu.roll(perr[...], (S - LIVE * m) % S, 1)[:, 0:PAD]
    meta_out[0:2, :] = jnp.where(valid, rolled[0:2], 0.0)
    meta_out[2:4, :] = rowmeta[0:2, :]
    meta_out[4:8, :] = jnp.zeros((4, PAD), F32)
    square = rolled[2:3] * rolled[2:3] + rolled[3:4] * rolled[3:4]
    square = jnp.where(valid, square, 0.0)
    chosen = iota((DEVICES, PAD), 0).astype(F32) == rowmeta[2:3, :]
    loss_col = jnp.sum(jnp.where(chosen, square, 0.0), axis=1, keepdims=True)
    count_col = jnp.sum(jnp.where(chosen, 1.0, 0.0), axis=1, keepdims=True)
    loss_row = jnp.broadcast_to(loss_col, (DEVICES, DEVICES)).T[0:1]
    count_row = jnp.broadcast_to(count_col, (DEVICES, DEVICES)).T[0:1]

    def back(q, _):
        rows = pl.ds(pl.multiple_of(q * JT, JT), JT)
        wc = jnp.concatenate([w[0, q].reshape(JT, 128), w[1, q].reshape(JT, 128)], axis=1)
        acc = jnp.zeros((16, JT), F32)
        for s in range(NCH):
            sl = slice(CH * s, CH * s + CH)
            act = t[rows, sl]
            bf = (nn(wc, bst[:, sl]) * (1.0 - act * act)).astype(BF)
            acc = acc + nt(feats[:, sl], bf)
        gwp[:, rows] = acc
        return 0

    lax.fori_loop(0, H // JT, back, 0)
    gwp[12:16, :] = jnp.zeros((4, H), F32)
    gwp[12:13, 0:DEVICES] = loss_row
    gwp[13:14, 0:DEVICES] = count_row

    g1 = [
        send(gwp.at[:, pl.ds(pl.multiple_of(mm * COLS, COLS), COLS)], rg.at[i], to)
        for i, (mm, to) in enumerate(members)
    ]
    for copy in s1a + s1b:
        copy.wait()
    gm[0, :, x] = gm[0, :, x] + ra[0] + ra[1] + ra[2]
    gm[1, yq] = gm[1, yq] + rb[0] + rb[1] + rb[2]
    s2 = [send(gm.at[0, yy, x], r2a.at[i], to) for i, (yy, to) in enumerate(ys)]
    s2 += [send(gm.at[1, yq, xx], r2b.at[i], to) for i, (xx, to) in enumerate(xs)]

    my_cols = pl.ds(pl.multiple_of(m * COLS, COLS), COLS)
    for copy in g1:
        copy.wait()
    part = gwp[:, my_cols]
    for i in range(7):
        part = part + rg[i]
    rgp[yq * 4 + x] = part
    g2 = [send(rgp.at[yq * 4 + x], rgp.at[yq * 4 + x], to) for to in plane]

    for copy in s2:
        copy.wait()
    fin[0] = gm[0, yq, x] + r2a[0] + r2a[1] + r2a[2]
    fin[1] = gm[1, yq, x] + r2b[0] + r2b[1] + r2b[2]
    s3 = [
        send(fin.at[:, pl.ds(pl.multiple_of(mm * 16, 16), 16), :], gmid_out.at[m], to)
        for mm, to in members
    ]
    gmid_out[m] = fin[:, mine, :]

    for copy in g2:
        copy.wait()
    part = rgp[0]
    for i in range(1, 16):
        part = part + rgp[i]
    small_out[m] = part
    g4 = [send(small_out.at[m], small_out.at[m], to) for _, to in members]
    for copy in s3 + g4 + halos:
        copy.wait()


N_SENDS = 7 + 7 + 6 + 18 + 2 + 28 + 12 + 3 + 6 + 7 + 7 + 15 + 7


def train(flow, counts, routes, index, win, wmid, wout):
    vm = pl.BlockSpec(memory_space=pltpu.VMEM)
    sds = jax.ShapeDtypeStruct
    return pl.pallas_call(
        train_kernel,
        out_shape=(
            sds((2, 5, 8, 512), F32),
            sds((8, PAD), F32),
            sds((GROUP, 16, COLS), F32),
            sds((GROUP, 2, 16, 128), F32),
        ),
        in_specs=[pl.BlockSpec(memory_space=pl.ANY)] * 7,
        out_specs=(pl.BlockSpec(memory_space=pl.ANY), vm, vm, vm),
        scratch_shapes=[
            pltpu.VMEM((H, S), F32),
            pltpu.VMEM((H, 1920), BF),
            pltpu.VMEM((2, 4, 4, 128, 128), BF),
            pltpu.VMEM((COLS, H), BF),
            pltpu.VMEM((COLS, S), F32),
            pltpu.VMEM((COLS, S), BF),
            pltpu.VMEM((2, 4, 4, 128, 128), F32),
            pltpu.VMEM((3, 4, 128, 128), F32),
            pltpu.VMEM((3, 4, 128, 128), F32),
            pltpu.VMEM((3, 128, 128), F32),
            pltpu.VMEM((3, 128, 128), F32),
            pltpu.VMEM((2, 128, 128), F32),
            pltpu.VMEM((4, 3, 32, 512), F32),
            pltpu.VMEM((2, 2, 32, 512), F32),
            pltpu.VMEM((GROUP, 2, 16, 128), BF),
            pltpu.VMEM((H, 16), BF),
            pltpu.VMEM((16, COLS), F32),
            pltpu.VMEM((2, 5, 8, 512), F32),
            pltpu.VMEM((GROUP, 16, PAD), BF),
            pltpu.VMEM((16, S + 128), F32),
            pltpu.VMEM((16, S), BF),
            pltpu.VMEM((GROUP, len(PARTS), 2, CH), F32),
            pltpu.VMEM((8, PAD), F32),
            pltpu.VMEM((8, S), F32),
            pltpu.VMEM((16, H), F32),
            pltpu.VMEM((7, 16, COLS), F32),
            pltpu.VMEM((16, 16, COLS), F32),
            pltpu.VMEM((1, TILES), jnp.int32),
            pltpu.VMEM((1, TILES), jnp.int32),
            pltpu.VMEM((CAP, TILES), jnp.int32),
            pltpu.VMEM((12, H), BF),
            pltpu.VMEM((16, H), BF),
            pltpu.VMEM((2, H), BF),
            pltpu.VMEM((16, TILES), F32),
            pltpu.SemaphoreType.DMA((11,)),
            pltpu.SemaphoreType.DMA((N_SENDS,)),
            pltpu.SemaphoreType.DMA((N_SENDS,)),
        ],
        compiler_params=pltpu.CompilerParams(
            collective_id=0, has_side_effects=True, vmem_limit_bytes=62 * 2**20
        ),
        name="train",
    )(flow, counts, routes.reshape(1, TILES), index.T, win, wmid, wout)


def slab_kernel(flow, diff, stress, halo, meta, small, gmid, field, new_stress, loss, gw, gwm):
    v = pl.program_id(0)

    @pl.when(v == 0)
    def _():
        zrow, xrow = meta[2:3, :], meta[3:4, :]
        oz = jnp.where(iota((32, PAD), 0).astype(F32) == zrow, 1.0, 0.0)
        ox = jnp.where(iota((PAD, PAD), 0).astype(F32) == xrow, 1.0, 0.0).astype(BF)
        lhs = jnp.concatenate([oz * meta[0:1, :], oz * meta[1:2, :], oz], axis=0).astype(BF)
        spread = nt(lhs, ox)
        hit = spread[64:96] > 0.5
        new_stress[0] = jnp.where(hit, spread[0:32], stress[0])
        new_stress[1] = jnp.where(hit, spread[32:64], stress[1])
        me = lax.axis_index("sec") * 64 + lax.axis_index("dev")
        ratio = 0.5 * small[0, 12:13, 0:DEVICES] / small[0, 13:14, 0:DEVICES]
        loss[0] = jnp.sum(jnp.where(iota((1, DEVICES), 1) == me, ratio, 0.0))
        for i in range(GROUP):
            gw[:, COLS * i:COLS * i + COLS] = small[i, 0:12, :]
            for h in range(2):
                at = COLS * i + 128 * h
                gwm[:, at:at + 128] = gmid[i, h]

    u = flow[0]
    row, col = iota((8, 32, 512), 1), iota((8, 32, 512), 2)
    below_z = jnp.where(row == 0, halo[0, v][:, None, :], pltpu.roll(u, 1, 1))
    above_z = jnp.where(row == 31, halo[1, v][:, None, :], pltpu.roll(u, 31, 1))
    below_x = jnp.where(col == 0, u, pltpu.roll(u, 1, 2))
    above_x = jnp.where(col == 511, u, pltpu.roll(u, 511, 2))
    below_y = jnp.concatenate([u[0:1], u[0:7]], axis=0)
    above_y = jnp.concatenate([u[1:8], u[7:8]], axis=0)
    spread = below_x + above_x + below_y + above_y + below_z + above_z - 6.0 * u
    field[0] = u + ADVECT * (below_x - u) + diff[...] * spread

    @pl.when(v == 1)
    def _():
        field[0, 0] = field[0, 0] - GAIN * new_stress[0]

    @pl.when(v == 3)
    def _():
        field[0, 0] = field[0, 0] - GAIN * new_stress[1]


def slab(flow, diff, stress, halo, meta, small, gmid):
    sds = jax.ShapeDtypeStruct

    def whole(shape):
        return pl.BlockSpec(shape, lambda v: (0,) * len(shape))

    block = pl.BlockSpec((1, 8, 32, 512), lambda v: (v, 0, 0, 0))
    return pl.pallas_call(
        slab_kernel,
        grid=(5,),
        out_shape=(
            sds((5, 8, 32, 512), F32),
            sds((2, 32, 512), F32),
            sds((1,), F32),
            sds((12, H), F32),
            sds((16, H), F32),
        ),
        in_specs=[
            block, whole((8, 32, 512)), whole((2, 32, 512)), whole((2, 5, 8, 512)),
            whole((8, PAD)), whole((GROUP, 16, COLS)), whole((GROUP, 2, 16, 128)),
        ],
        out_specs=(
            block, whole((2, 32, 512)), pl.BlockSpec(memory_space=pltpu.SMEM),
            whole((12, H)), whole((16, H)),
        ),
        compiler_params=pltpu.CompilerParams(vmem_limit_bytes=62 * 2**20),
        name="slab",
    )(flow, diff, stress, halo, meta, small, gmid)


def body(flow, diff, stress, counts, routes, index, win, wmid, wout):
    halo, meta, small, gmid = train(flow, counts, routes, index, win, wmid, wout)
    return slab(flow, diff, stress, halo, meta, small, gmid)


def solution(mesh):
    both = ("sec", "dev")
    in_specs = (
        P(None, None, both, None), P(None, both, None), P(None, both, None),
        P(both, None), P(both, None), P(both, None), P(), P(both, None), P(),
    )
    out_specs = (P(None, None, both, None), P(None, both, None), P(both), P(), P(both, None))
    return jax.shard_map(body, mesh=mesh, in_specs=in_specs, out_specs=out_specs, check_vma=False)
```

```python
import math

import jax
import jax.numpy as jnp
from jax import lax
from jax.experimental import pallas as pl
from jax.experimental.pallas import tpu as pltpu
from jax.sharding import PartitionSpec as P

BF = jnp.bfloat16
F32 = jnp.float32
MESH = pl.DeviceIdType.MESH

H = 2048
CAP = 4
TILES = 192
LIVE = 480
PAD = 512
GROUP = 8
COLS = H // GROUP
S = GROUP * LIVE
CH = 1280
NCH = S // CH
PARTS = ((0, 1280, 0), (1280, 640, 1280), (1920, 1280, 0), (3200, 640, 1280))
JT = 512
DEVICES = 128
ADVECT = 0.3
GAIN = 0.5
SCALE = 32.0 / math.sqrt(LIVE * DEVICES)


def nn(a, b):
    return jnp.dot(a, b, preferred_element_type=F32)


def nt(a, b):
    return lax.dot_general(a, b, (((1,), (1,)), ((), ())), preferred_element_type=F32)


def tn(a, b):
    return lax.dot_general(a, b, (((0,), (0,)), ((), ())), preferred_element_type=F32)


def iota(shape, dim):
    return lax.broadcasted_iota(jnp.int32, shape, dim)


def train_kernel(
    flow, flat_flow, diff_h, counts_h, routes_h, index_h, win_h, wmid_h, wout_h,
    adv_out, meta_out, small_out, gmid_out,
    t, fs, w, wct, d2, bst, gm, ra, rb, r2a, r2b, fin,
    planes, tplanes, halo, wsrc, wint, wpad, own, fbuf, ftot, feats, pbuf, rowmeta, perr,
    gwp, rg, rgp, counts, routes, index, win, wmid, wout, table, metav, smallv,
    lsem, ssem, rsem,
):
    sec = lax.axis_index("sec")
    dev = lax.axis_index("dev")
    m = dev % 8
    x = (dev // 8) % 4
    yh = dev // 32
    y = yh * 2 + sec
    yq = sec * 2 + yh
    flat = sec * 64 + dev
    used = [0]

    def send(src, dst, to):
        i = used[0]
        used[0] += 1
        copy = pltpu.make_async_remote_copy(
            src_ref=src, dst_ref=dst, send_sem=ssem.at[i], recv_sem=rsem.at[i],
            device_id=to, device_id_type=MESH,
        )
        copy.start()
        return copy

    def at_plane(yy, xx):
        return (yy % 2, (yy // 2) * 32 + xx * 8 + m)

    members = [((m + k) % 8, (sec, dev - m + (m + k) % 8)) for k in range(1, 8)]
    xs = [((x + k) % 4, at_plane(y, (x + k) % 4)) for k in (1, 3, 2)]
    ys = []
    for k in (1, 3, 2):
        yy = (y + k) % 4
        ys.append(((yy % 2) * 2 + yy // 2, at_plane(yy, x)))
    plane = [
        at_plane((y + a) % 4, (x + b) % 4) for a in range(4) for b in range(4) if a or b
    ]
    up = (flat + 1) % 128
    down = (flat + 127) % 128
    up_id = (up // 64, up % 64)
    down_id = (down // 64, down % 64)

    barrier = pltpu.get_barrier_semaphore()
    partners = [p for _, p in members] + plane + [up_id, down_id]
    for p in partners:
        pl.semaphore_signal(barrier, inc=1, device_id=p, device_id_type=MESH)

    pairs = [
        (wmid_h, wmid), (counts_h, counts), (routes_h, routes), (index_h, index),
        (win_h, win), (wout_h, wout),
        (flow.at[0:4, 0:3], planes), (flow.at[1, 3:5], tplanes.at[0]),
        (flow.at[3, 3:5], tplanes.at[1]), (flow.at[:, :, 0, :], own.at[0]),
        (flow.at[:, :, 31, :], own.at[1]),
    ]
    loads = [pltpu.make_async_copy(a, b, lsem.at[i]) for i, (a, b) in enumerate(pairs)]
    for copy in loads:
        copy.start()
    loads[0].wait()

    for i in range(GROUP):
        for h in range(2):
            wsrc[i, h] = wmid[:, COLS * i + 128 * h:COLS * i + 128 * h + 128]
    for copy in loads[1:6]:
        copy.wait()
    winp = jnp.concatenate([win[...].astype(F32), jnp.zeros((4, H), F32)], axis=0)
    wint[...] = winp.T.astype(BF)
    wpad[...] = jnp.zeros_like(wpad)
    wpad[0:2, :] = wout[:, pl.ds(pl.multiple_of(m * COLS, COLS), COLS)].astype(F32)

    cnt = jnp.broadcast_to(counts[...].astype(F32), (16, TILES)).astype(BF)
    r_i, c_i = iota((TILES, TILES), 0), iota((TILES, TILES), 1)
    start = nt((c_i < r_i).astype(F32).astype(BF), cnt)[:, 0:1]
    ends = nt((c_i <= r_i).astype(F32).astype(BF), cnt)[:, 0:1]
    start_row = nn(cnt, (r_i < c_i).astype(F32).astype(BF))[0:1].astype(jnp.int32)
    place = iota((TILES, PAD), 1).astype(F32)
    onehot = jnp.where((place >= start) & (place < ends), 1.0, 0.0).astype(BF)
    idx = index[...]
    table[...] = jnp.zeros_like(table)
    table[0:4, :] = (idx >> 9).astype(F32)
    table[4:8, :] = ((idx >> 4) & 31).astype(F32)
    table[8:12, :] = (idx & 15).astype(F32)
    table[12:13, :] = (start_row >> 4).astype(F32)
    table[13:14, :] = (start_row & 15).astype(F32)
    table[14:15, :] = routes[...].astype(F32)
    vals = nn(table[...].astype(BF), onehot)
    lane = iota((1, PAD), 1)
    kk = lane.astype(F32) - (vals[12:13] * 16.0 + vals[13:14])
    zrow = jnp.zeros((1, PAD), F32)
    xrow = jnp.zeros((1, PAD), F32)
    for k in range(CAP):
        hit = kk == float(k)
        zrow = jnp.where(hit, vals[k:k + 1], zrow)
        xrow = jnp.where(hit, vals[4 + k:5 + k] * 16.0 + vals[8 + k:9 + k], xrow)
    valid = lane < LIVE
    zrow = jnp.where(valid, zrow, -1.0)
    xrow = jnp.where(valid, xrow, -1.0)
    rowmeta[0:1, :] = zrow
    rowmeta[1:2, :] = xrow
    rowmeta[2:3, :] = jnp.where(valid, vals[14:15], -1.0)
    oz = jnp.where(iota((32, PAD), 0).astype(F32) == zrow, 1.0, 0.0)
    ox = jnp.where(iota((PAD, PAD), 0).astype(F32) == xrow, 1.0, 0.0).astype(BF)
    for copy in loads[6:]:
        copy.wait()
    tp = jnp.stack([tplanes[0, 1] - tplanes[0, 0], tplanes[1, 1] - tplanes[1, 0]])
    table_p = jnp.concatenate(
        [planes[...].reshape(384, PAD).astype(BF), tp.reshape(64, PAD).astype(BF)], axis=0
    )
    got = nn(table_p, ox).reshape(14, 32, PAD) * oz[None]
    picked = jnp.sum(got, axis=1)
    picked = jnp.concatenate([picked, jnp.zeros((2, PAD), F32)], axis=0)
    fbuf[m] = picked.astype(BF)

    pl.semaphore_wait(barrier, len(partners))

    mine = pl.ds(pl.multiple_of(m * 16, 16), 16)
    w0 = [send(wsrc.at[mm], w.at[:, yq, x, mine, :], to) for mm, to in members]
    w[:, yq, x, mine, :] = wsrc[m]
    fcopies = [send(fbuf.at[m], fbuf.at[m], to) for _, to in members]
    for copy in w0:
        copy.wait()
    w1x = [send(w.at[:, yq, x], w.at[:, yq, x], to) for _, to in xs]
    w1y = [send(w.at[:, yq, x], w.at[:, yq, x], to) for _, to in ys]
    for copy in fcopies:
        copy.wait()
    ftot[...] = jnp.zeros_like(ftot)
    for i in range(GROUP):
        base, rest = divmod(LIVE * i, 128)
        wide = jnp.concatenate([fbuf[i].astype(F32), jnp.zeros((16, 128), F32)], axis=1)
        if rest:
            wide = pltpu.roll(wide, rest, 1)
        ftot[:, 128 * base:128 * base + PAD + 128] += wide
    feats[...] = ftot[:, 0:S].astype(BF)

    w2 = []
    for i, k in enumerate((1, 3, 2)):
        w1x[i].wait()
        xx = (x + 4 - k) % 4
        w2 += [send(w.at[0, yq, xx], w.at[0, yq, xx], to) for _, to in ys]
        w1y[i].wait()
        yy = (y + 4 - k) % 4
        qq = (yy % 2) * 2 + yy // 2
        w2 += [send(w.at[1, qq, x], w.at[1, qq, x], to) for _, to in xs]
    halos = [
        send(own.at[0], halo.at[1], down_id),
        send(own.at[1], halo.at[0], up_id),
    ]

    def first(q):
        at, size, slot = PARTS[q]
        sl = slice(at, at + size)

        def inner(j, _):
            rows = pl.ds(pl.multiple_of(j * JT, JT), JT)
            act = jnp.tanh(nn(wint[rows, :], feats[:, sl]))
            t[rows, sl] = act
            fs[rows, slot:slot + size] = act.astype(BF)
            return 0

        lax.fori_loop(0, H // JT, inner, 0, unroll=True)

    pcopies = []

    def second(q):
        at, size, slot = PARTS[q]
        act2 = jnp.tanh(nn(wct[...], fs[:, slot:slot + size]))
        d2[:, at:at + size] = 1.0 - act2 * act2
        pbuf[m, q, :, 0:size] = nn(wpad[...].astype(BF), act2.astype(BF))[0:2]
        ref = pbuf.at[m, q, :, 0:size]
        pcopies.append([send(ref, ref, to) for _, to in members])

    first(0)
    first(1)
    for copy in w2:
        copy.wait()
    for h in range(2):
        wct[128 * h:128 * h + 128, :] = w[h].reshape(H, 128).astype(F32).T.astype(BF)
    second(0)
    first(2)
    second(1)
    first(3)
    second(2)
    second(3)
    perr[4:8, :] = jnp.zeros((4, S), F32)
    for q, (at, size, _) in enumerate(PARTS):
        sl = slice(at, at + size)
        for copy in pcopies[q]:
            copy.wait()
        pred = pbuf[0, q, :, 0:size]
        for i in range(1, GROUP):
            pred = pred + pbuf[i, q, :, 0:size]
        err = pred - ftot[12:14, sl]
        perr[0:2, sl] = pred
        perr[2:4, sl] = err
        bo = jnp.concatenate([err * SCALE, jnp.zeros((14, size), F32)], axis=0).astype(BF)
        bst[:, sl] = (tn(wpad[...].astype(BF), bo) * d2[:, sl]).astype(BF)

    s1a = []
    s1b = []
    for n, k in enumerate((1, 3, 2, 0)):
        yy = (y + k) % 4
        q = (yy % 2) * 2 + yy // 2
        rows = pl.ds(pl.multiple_of(q * JT, JT), JT)
        part = nt(t[rows, :].astype(BF), bst[...])
        for h in range(2):
            gm[h, q] = part[:, 128 * h:128 * h + 128].reshape(4, 128, 128)
        if k:
            s1b.append(send(gm.at[1, q], rb.at[n], ys[n][1]))
        for i, (xx, to) in enumerate(xs):
            s1a.append(send(gm.at[0, q, xx], ra.at[i, q], to))

    rolled = pltpu.roll(perr[...], (S - LIVE * m) % S, 1)[:, 0:PAD]
    metav[0:2, :] = jnp.where(valid, rolled[0:2], 0.0)
    metav[2:4, :] = rowmeta[0:2, :]
    metav[4:8, :] = jnp.zeros((4, PAD), F32)
    stores = [pltpu.make_async_copy(metav, meta_out, lsem.at[18])]
    stores[0].start()
    square = rolled[2:3] * rolled[2:3] + rolled[3:4] * rolled[3:4]
    square = jnp.where(valid, square, 0.0)
    chosen = iota((DEVICES, PAD), 0).astype(F32) == rowmeta[2:3, :]
    loss_col = jnp.sum(jnp.where(chosen, square, 0.0), axis=1, keepdims=True)
    count_col = jnp.sum(jnp.where(chosen, 1.0, 0.0), axis=1, keepdims=True)
    loss_row = jnp.broadcast_to(loss_col, (DEVICES, DEVICES)).T[0:1]
    count_row = jnp.broadcast_to(count_col, (DEVICES, DEVICES)).T[0:1]

    def back(q, _):
        rows = pl.ds(pl.multiple_of(q * JT, JT), JT)
        wc = jnp.concatenate([w[0, q].reshape(JT, 128), w[1, q].reshape(JT, 128)], axis=1)
        acc = jnp.zeros((16, JT), F32)
        for s in range(NCH):
            sl = slice(CH * s, CH * s + CH)
            act = t[rows, sl]
            bf = (nn(wc, bst[:, sl]) * (1.0 - act * act)).astype(BF)
            acc = acc + nt(feats[:, sl], bf)
        gwp[:, rows] = acc
        return 0

    lax.fori_loop(0, H // JT - 1, back, 0)
    slab_loads = [
        pltpu.make_async_copy(flat_flow, t.at[0:1280, 0:512], lsem.at[11]),
        pltpu.make_async_copy(diff_h, t.at[0:256, 512:1024], lsem.at[12]),
    ]
    for copy in slab_loads:
        copy.start()
    back(H // JT - 1, 0)
    gwp[12:16, :] = jnp.zeros((4, H), F32)
    gwp[12:13, 0:DEVICES] = loss_row
    gwp[13:14, 0:DEVICES] = count_row

    def stencil(v):
        row, col = iota((32, 512), 0), iota((32, 512), 1)
        for l in range(8):
            at = v * 256 + l * 32
            u = t[at:at + 32, 0:512]
            low, high = halo[0, v, l:l + 1, :], halo[1, v, l:l + 1, :]
            below_z = jnp.where(row == 0, low, pltpu.roll(u, 1, 0))
            above_z = jnp.where(row == 31, high, pltpu.roll(u, 31, 0))
            below_x = jnp.where(col == 0, u, pltpu.roll(u, 1, 1))
            above_x = jnp.where(col == 511, u, pltpu.roll(u, 511, 1))
            below_y = t[at - 32:at, 0:512] if l > 0 else u
            above_y = t[at + 32:at + 64, 0:512] if l < 7 else u
            spread = below_x + above_x + below_y + above_y + below_z + above_z - 6.0 * u
            value = u + ADVECT * (below_x - u) + t[l * 32:l * 32 + 32, 512:1024] * spread
            t[at:at + 32, 1024:1536] = value
        rows = slice(v * 256, v * 256 + 256)
        copy = pltpu.make_async_copy(t.at[rows, 1024:1536], adv_out.at[rows, :], lsem.at[13 + v])
        copy.start()
        stores.append(copy)

    g1 = [
        send(gwp.at[:, pl.ds(pl.multiple_of(mm * COLS, COLS), COLS)], rg.at[i], to)
        for i, (mm, to) in enumerate(members)
    ]
    for copy in s1a + s1b + halos + slab_loads:
        copy.wait()
    gm[0, :, x] = gm[0, :, x] + ra[0] + ra[1] + ra[2]
    gm[1, yq] = gm[1, yq] + rb[0] + rb[1] + rb[2]
    s2 = [send(gm.at[0, yy, x], r2a.at[i], to) for i, (yy, to) in enumerate(ys)]
    s2 += [send(gm.at[1, yq, xx], r2b.at[i], to) for i, (xx, to) in enumerate(xs)]

    stencil(0)
    my_cols = pl.ds(pl.multiple_of(m * COLS, COLS), COLS)
    stencil(1)
    for copy in g1:
        copy.wait()
    part = gwp[:, my_cols]
    for i in range(7):
        part = part + rg[i]
    rgp[yq * 4 + x] = part
    g2 = [send(rgp.at[yq * 4 + x], rgp.at[yq * 4 + x], to) for to in plane]

    stencil(2)
    for copy in s2:
        copy.wait()
    fin[0] = gm[0, yq, x] + r2a[0] + r2a[1] + r2a[2]
    fin[1] = gm[1, yq, x] + r2b[0] + r2b[1] + r2b[2]
    s3 = [
        send(fin.at[:, pl.ds(pl.multiple_of(mm * 16, 16), 16), :], gmid_out.at[m], to)
        for mm, to in members
    ]
    stores.append(pltpu.make_async_copy(fin.at[:, mine, :], gmid_out.at[m], lsem.at[19]))
    stores[-1].start()
    stencil(3)

    for copy in g2:
        copy.wait()
    part = rgp[0]
    for i in range(1, 16):
        part = part + rgp[i]
    smallv[...] = part
    g4 = [send(smallv, small_out.at[m], to) for _, to in members]
    stores.append(pltpu.make_async_copy(smallv, small_out.at[m], lsem.at[20]))
    stores[-1].start()
    stencil(4)
    for copy in s3 + g4 + stores:
        copy.wait()


N_SENDS = 7 + 7 + 6 + 18 + 2 + 28 + 12 + 3 + 6 + 7 + 7 + 15 + 7


def train(flow, diff, counts, routes, index, win, wmid, wout):
    sds = jax.ShapeDtypeStruct
    return pl.pallas_call(
        train_kernel,
        out_shape=(
            sds((1280, 512), F32),
            sds((8, PAD), F32),
            sds((GROUP, 16, COLS), F32),
            sds((GROUP, 2, 16, 128), F32),
        ),
        in_specs=[pl.BlockSpec(memory_space=pl.ANY)] * 9,
        out_specs=(pl.BlockSpec(memory_space=pl.ANY),) * 4,
        scratch_shapes=[
            pltpu.VMEM((H, S), F32),
            pltpu.VMEM((H, 1920), BF),
            pltpu.VMEM((2, 4, 4, 128, 128), BF),
            pltpu.VMEM((COLS, H), BF),
            pltpu.VMEM((COLS, S), F32),
            pltpu.VMEM((COLS, S), BF),
            pltpu.VMEM((2, 4, 4, 128, 128), F32),
            pltpu.VMEM((3, 4, 128, 128), F32),
            pltpu.VMEM((3, 4, 128, 128), F32),
            pltpu.VMEM((3, 128, 128), F32),
            pltpu.VMEM((3, 128, 128), F32),
            pltpu.VMEM((2, 128, 128), F32),
            pltpu.VMEM((4, 3, 32, 512), F32),
            pltpu.VMEM((2, 2, 32, 512), F32),
            pltpu.VMEM((2, 5, 8, 512), F32),
            pltpu.VMEM((GROUP, 2, 16, 128), BF),
            pltpu.VMEM((H, 16), BF),
            pltpu.VMEM((16, COLS), F32),
            pltpu.VMEM((2, 5, 8, 512), F32),
            pltpu.VMEM((GROUP, 16, PAD), BF),
            pltpu.VMEM((16, S + 128), F32),
            pltpu.VMEM((16, S), BF),
            pltpu.VMEM((GROUP, len(PARTS), 2, CH), F32),
            pltpu.VMEM((8, PAD), F32),
            pltpu.VMEM((8, S), F32),
            pltpu.VMEM((16, H), F32),
            pltpu.VMEM((7, 16, COLS), F32),
            pltpu.VMEM((16, 16, COLS), F32),
            pltpu.VMEM((1, TILES), jnp.int32),
            pltpu.VMEM((1, TILES), jnp.int32),
            pltpu.VMEM((CAP, TILES), jnp.int32),
            pltpu.VMEM((12, H), BF),
            pltpu.VMEM((16, H), BF),
            pltpu.VMEM((2, H), BF),
            pltpu.VMEM((16, TILES), F32),
            pltpu.VMEM((8, PAD), F32),
            pltpu.VMEM((16, COLS), F32),
            pltpu.SemaphoreType.DMA((21,)),
            pltpu.SemaphoreType.DMA((N_SENDS,)),
            pltpu.SemaphoreType.DMA((N_SENDS,)),
        ],
        compiler_params=pltpu.CompilerParams(
            collective_id=0, has_side_effects=True, vmem_limit_bytes=62 * 2**20
        ),
        name="train",
    )(flow, flow.reshape(1280, 512), diff.reshape(256, 512), counts, routes.reshape(1, TILES), index.T, win, wmid, wout)


def finish_kernel(
    adv, stress_h, meta_h, small_h, gmid_h, field, new_stress, loss, gw, gwm,
    held, stress, meta, small, gmid, wall, gwv, gwmv, sem,
):
    order = (1, 3, 0, 2, 4)
    first = [
        pltpu.make_async_copy(meta_h, meta, sem.at[10]),
        pltpu.make_async_copy(stress_h, stress, sem.at[11]),
    ]
    then = [
        pltpu.make_async_copy(small_h, small, sem.at[12]),
        pltpu.make_async_copy(gmid_h, gmid, sem.at[13]),
    ]
    loads = {v: pltpu.make_async_copy(adv.at[v], held.at[v], sem.at[v]) for v in order}
    stores = {v: pltpu.make_async_copy(held.at[v], field.at[v], sem.at[5 + v]) for v in order}
    last = [
        pltpu.make_async_copy(wall, new_stress, sem.at[14]),
        pltpu.make_async_copy(gwv, gw, sem.at[15]),
        pltpu.make_async_copy(gwmv, gwm, sem.at[16]),
    ]
    for copy in first + [loads[v] for v in order] + then:
        copy.start()
    first[0].wait()
    zrow, xrow = meta[2:3, :], meta[3:4, :]
    oz = jnp.where(iota((32, PAD), 0).astype(F32) == zrow, 1.0, 0.0)
    ox = jnp.where(iota((PAD, PAD), 0).astype(F32) == xrow, 1.0, 0.0).astype(BF)
    lhs = jnp.concatenate([oz * meta[0:1, :], oz * meta[1:2, :], oz], axis=0).astype(BF)
    spread = nt(lhs, ox)
    hit = spread[64:96] > 0.5
    first[1].wait()
    for v in (0, 2, 4):
        loads[v].wait()
        stores[v].start()
    for i, v in enumerate((1, 3)):
        value = jnp.where(hit, spread[32 * i:32 * i + 32], stress[i])
        wall[i] = value
        loads[v].wait()
        held[v, 0] = held[v, 0] - GAIN * value
        stores[v].start()
    last[0].start()
    for copy in then:
        copy.wait()
    for i in range(GROUP):
        gwv[:, COLS * i:COLS * i + COLS] = small[i, 0:12, :]
        for h in range(2):
            at = COLS * i + 128 * h
            gwmv[:, at:at + 128] = gmid[i, h]
    last[1].start()
    last[2].start()
    me = lax.axis_index("sec") * 64 + lax.axis_index("dev")
    ratio = 0.5 * small[0, 12:13, 0:DEVICES] / small[0, 13:14, 0:DEVICES]
    loss[0] = jnp.sum(jnp.where(iota((1, DEVICES), 1) == me, ratio, 0.0))
    for copy in [stores[v] for v in order] + last:
        copy.wait()


def finish(adv, stress, meta, small, gmid):
    sds = jax.ShapeDtypeStruct
    anywhere = pl.BlockSpec(memory_space=pl.ANY)
    return pl.pallas_call(
        finish_kernel,
        out_shape=(
            sds((5, 8, 32, 512), F32),
            sds((2, 32, 512), F32),
            sds((1,), F32),
            sds((12, H), F32),
            sds((16, H), F32),
        ),
        in_specs=[anywhere] * 5,
        out_specs=(anywhere, anywhere, pl.BlockSpec(memory_space=pltpu.SMEM), anywhere, anywhere),
        scratch_shapes=[
            pltpu.VMEM((5, 8, 32, 512), F32),
            pltpu.VMEM((2, 32, 512), F32),
            pltpu.VMEM((8, PAD), F32),
            pltpu.VMEM((GROUP, 16, COLS), F32),
            pltpu.VMEM((GROUP, 2, 16, 128), F32),
            pltpu.VMEM((2, 32, 512), F32),
            pltpu.VMEM((12, H), F32),
            pltpu.VMEM((16, H), F32),
            pltpu.SemaphoreType.DMA((17,)),
        ],
        compiler_params=pltpu.CompilerParams(vmem_limit_bytes=62 * 2**20),
        name="finish",
    )(adv.reshape(5, 8, 32, 512), stress, meta, small, gmid)


def body(flow, diff, stress, counts, routes, index, win, wmid, wout):
    adv, meta, small, gmid = train(flow, diff, counts, routes, index, win, wmid, wout)
    return finish(adv, stress, meta, small, gmid)


def solution(mesh):
    both = ("sec", "dev")
    in_specs = (
        P(None, None, both, None), P(None, both, None), P(None, both, None),
        P(both, None), P(both, None), P(both, None), P(), P(both, None), P(),
    )
    out_specs = (P(None, None, both, None), P(None, both, None), P(both), P(), P(both, None))
    return jax.shard_map(body, mesh=mesh, in_specs=in_specs, out_specs=out_specs, check_vma=False)
```

```python
import math

import jax
import jax.numpy as jnp
from jax import lax
from jax.experimental import pallas as pl
from jax.experimental.pallas import tpu as pltpu
from jax.sharding import PartitionSpec as P

BF = jnp.bfloat16
F32 = jnp.float32
MESH = pl.DeviceIdType.MESH

H = 2048
CAP = 4
TILES = 192
LIVE = 480
PAD = 512
GROUP = 8
COLS = H // GROUP
S = GROUP * LIVE
CH = 1280
NCH = S // CH
PARTS = ((0, 1280, 0), (1280, 640, 1280), (1920, 1280, 0), (3200, 640, 1280))
JT = 512
DEVICES = 128
ADVECT = 0.3
GAIN = 0.5
SCALE = 32.0 / math.sqrt(LIVE * DEVICES)


def nn(a, b):
    return jnp.dot(a, b, preferred_element_type=F32)


def nt(a, b):
    return lax.dot_general(a, b, (((1,), (1,)), ((), ())), preferred_element_type=F32)


def tn(a, b):
    return lax.dot_general(a, b, (((0,), (0,)), ((), ())), preferred_element_type=F32)


def iota(shape, dim):
    return lax.broadcasted_iota(jnp.int32, shape, dim)


def train_kernel(
    flow, flat_flow, diff_h, counts_h, routes_h, index_h, win_h, wmid_h, wout_h,
    adv_out, meta_out, small_out, gmid_out,
    t, fs, w, wct, d2, bst, gm, ra, rb, r2a, r2b, fin,
    planes, tplanes, halo, wsrc, wint, wpad, own, fbuf, ftot, feats, pbuf, rowmeta, perr,
    gwp, rg, rgp, counts, routes, index, win, wmid, wout, table, metav, smallv,
    lsem, ssem, rsem,
):
    sec = lax.axis_index("sec")
    dev = lax.axis_index("dev")
    m = dev % 8
    x = (dev // 8) % 4
    yh = dev // 32
    y = yh * 2 + sec
    yq = sec * 2 + yh
    flat = sec * 64 + dev
    used = [0]

    def send(src, dst, to):
        i = used[0]
        used[0] += 1
        copy = pltpu.make_async_remote_copy(
            src_ref=src, dst_ref=dst, send_sem=ssem.at[i], recv_sem=rsem.at[i],
            device_id=to, device_id_type=MESH,
        )
        copy.start()
        return copy

    def at_plane(yy, xx):
        return (yy % 2, (yy // 2) * 32 + xx * 8 + m)

    members = [((m + k) % 8, (sec, dev - m + (m + k) % 8)) for k in range(1, 8)]
    xs = [((x + k) % 4, at_plane(y, (x + k) % 4)) for k in (1, 3, 2)]
    ys = []
    for k in (1, 3, 2):
        yy = (y + k) % 4
        ys.append(((yy % 2) * 2 + yy // 2, at_plane(yy, x)))
    plane = [
        at_plane((y + a) % 4, (x + b) % 4) for a in range(4) for b in range(4) if a or b
    ]
    up = (flat + 1) % 128
    down = (flat + 127) % 128
    up_id = (up // 64, up % 64)
    down_id = (down // 64, down % 64)

    barrier = pltpu.get_barrier_semaphore()
    partners = [p for _, p in members] + plane + [up_id, down_id]
    for p in partners:
        pl.semaphore_signal(barrier, inc=1, device_id=p, device_id_type=MESH)

    pairs = [
        (wmid_h, wmid), (counts_h, counts), (routes_h, routes), (index_h, index),
        (win_h, win), (wout_h, wout),
        (flow.at[0:4, 0:3], planes), (flow.at[1, 3:5], tplanes.at[0]),
        (flow.at[3, 3:5], tplanes.at[1]), (flow.at[:, :, 0, :], own.at[0]),
        (flow.at[:, :, 31, :], own.at[1]),
    ]
    loads = [pltpu.make_async_copy(a, b, lsem.at[i]) for i, (a, b) in enumerate(pairs)]
    for copy in loads:
        copy.start()
    loads[0].wait()

    for i in range(GROUP):
        for h in range(2):
            wsrc[i, h] = wmid[:, COLS * i + 128 * h:COLS * i + 128 * h + 128]
    for copy in loads[1:6]:
        copy.wait()

    cnt = jnp.broadcast_to(counts[...].astype(F32), (16, TILES)).astype(BF)
    r_i, c_i = iota((TILES, TILES), 0), iota((TILES, TILES), 1)
    start = nt((c_i < r_i).astype(F32).astype(BF), cnt)[:, 0:1]
    ends = nt((c_i <= r_i).astype(F32).astype(BF), cnt)[:, 0:1]
    start_row = nn(cnt, (r_i < c_i).astype(F32).astype(BF))[0:1].astype(jnp.int32)
    place = iota((TILES, PAD), 1).astype(F32)
    onehot = jnp.where((place >= start) & (place < ends), 1.0, 0.0).astype(BF)
    idx = index[...]
    table[...] = jnp.zeros_like(table)
    table[0:4, :] = (idx >> 9).astype(F32)
    table[4:8, :] = ((idx >> 4) & 31).astype(F32)
    table[8:12, :] = (idx & 15).astype(F32)
    table[12:13, :] = (start_row >> 4).astype(F32)
    table[13:14, :] = (start_row & 15).astype(F32)
    table[14:15, :] = routes[...].astype(F32)
    vals = nn(table[...].astype(BF), onehot)
    lane = iota((1, PAD), 1)
    kk = lane.astype(F32) - (vals[12:13] * 16.0 + vals[13:14])
    zrow = jnp.zeros((1, PAD), F32)
    xrow = jnp.zeros((1, PAD), F32)
    for k in range(CAP):
        hit = kk == float(k)
        zrow = jnp.where(hit, vals[k:k + 1], zrow)
        xrow = jnp.where(hit, vals[4 + k:5 + k] * 16.0 + vals[8 + k:9 + k], xrow)
    valid = lane < LIVE
    zrow = jnp.where(valid, zrow, -1.0)
    xrow = jnp.where(valid, xrow, -1.0)
    rowmeta[0:1, :] = zrow
    rowmeta[1:2, :] = xrow
    rowmeta[2:3, :] = jnp.where(valid, vals[14:15], -1.0)
    oz = jnp.where(iota((32, PAD), 0).astype(F32) == zrow, 1.0, 0.0)
    ox = jnp.where(iota((PAD, PAD), 0).astype(F32) == xrow, 1.0, 0.0).astype(BF)
    for copy in loads[6:]:
        copy.wait()
    tp = jnp.stack([tplanes[0, 1] - tplanes[0, 0], tplanes[1, 1] - tplanes[1, 0]])
    table_p = jnp.concatenate(
        [planes[...].reshape(384, PAD).astype(BF), tp.reshape(64, PAD).astype(BF)], axis=0
    )
    got = nn(table_p, ox).reshape(14, 32, PAD) * oz[None]
    picked = jnp.sum(got, axis=1)
    picked = jnp.concatenate([picked, jnp.zeros((2, PAD), F32)], axis=0)
    fbuf[m] = picked.astype(BF)

    pl.semaphore_wait(barrier, len(partners))

    mine = pl.ds(pl.multiple_of(m * 16, 16), 16)
    w0 = [send(wsrc.at[mm], w.at[:, yq, x, mine, :], to) for mm, to in members]
    w[:, yq, x, mine, :] = wsrc[m]
    fcopies = [send(fbuf.at[m], fbuf.at[m], to) for _, to in members]
    winp = jnp.concatenate([win[...].astype(F32), jnp.zeros((4, H), F32)], axis=0)
    wint[...] = winp.T.astype(BF)
    wpad[...] = jnp.zeros_like(wpad)
    wpad[0:2, :] = wout[:, pl.ds(pl.multiple_of(m * COLS, COLS), COLS)].astype(F32)
    for copy in w0:
        copy.wait()
    w1x = [send(w.at[:, yq, x], w.at[:, yq, x], to) for _, to in xs]
    w1y = [send(w.at[:, yq, x], w.at[:, yq, x], to) for _, to in ys]
    for copy in fcopies:
        copy.wait()
    ftot[...] = jnp.zeros_like(ftot)
    for i in range(GROUP):
        base, rest = divmod(LIVE * i, 128)
        wide = jnp.concatenate([fbuf[i].astype(F32), jnp.zeros((16, 128), F32)], axis=1)
        if rest:
            wide = pltpu.roll(wide, rest, 1)
        ftot[:, 128 * base:128 * base + PAD + 128] += wide
    feats[...] = ftot[:, 0:S].astype(BF)

    w2 = []
    for i, k in enumerate((1, 3, 2)):
        w1x[i].wait()
        xx = (x + 4 - k) % 4
        w2 += [send(w.at[0, yq, xx], w.at[0, yq, xx], to) for _, to in ys]
        w1y[i].wait()
        yy = (y + 4 - k) % 4
        qq = (yy % 2) * 2 + yy // 2
        w2 += [send(w.at[1, qq, x], w.at[1, qq, x], to) for _, to in xs]
    halos = [
        send(own.at[0], halo.at[1], down_id),
        send(own.at[1], halo.at[0], up_id),
    ]

    def first(q):
        at, size, slot = PARTS[q]
        sl = slice(at, at + size)

        def inner(j, _):
            rows = pl.ds(pl.multiple_of(j * JT, JT), JT)
            act = jnp.tanh(nn(wint[rows, :], feats[:, sl]))
            t[rows, sl] = act
            fs[rows, slot:slot + size] = act.astype(BF)
            return 0

        lax.fori_loop(0, H // JT, inner, 0, unroll=True)

    pcopies = []

    def second(q):
        at, size, slot = PARTS[q]
        act2 = jnp.tanh(nn(wct[...], fs[:, slot:slot + size]))
        d2[:, at:at + size] = 1.0 - act2 * act2
        pbuf[m, q, :, 0:size] = nn(wpad[...].astype(BF), act2.astype(BF))[0:2]
        ref = pbuf.at[m, q, :, 0:size]
        pcopies.append([send(ref, ref, to) for _, to in members])

    first(0)
    first(1)
    for copy in w2:
        copy.wait()
    for h in range(2):
        wct[128 * h:128 * h + 128, :] = w[h].reshape(H, 128).astype(F32).T.astype(BF)
    second(0)
    first(2)
    second(1)
    first(3)
    second(2)
    second(3)
    perr[4:8, :] = jnp.zeros((4, S), F32)
    for q, (at, size, _) in enumerate(PARTS):
        sl = slice(at, at + size)
        for copy in pcopies[q]:
            copy.wait()
        pred = pbuf[0, q, :, 0:size]
        for i in range(1, GROUP):
            pred = pred + pbuf[i, q, :, 0:size]
        err = pred - ftot[12:14, sl]
        perr[0:2, sl] = pred
        perr[2:4, sl] = err
        bo = jnp.concatenate([err * SCALE, jnp.zeros((14, size), F32)], axis=0).astype(BF)
        bst[:, sl] = (tn(wpad[...].astype(BF), bo) * d2[:, sl]).astype(BF)

    s1a = []
    s1b = []
    for n, k in enumerate((1, 3, 2, 0)):
        yy = (y + k) % 4
        q = (yy % 2) * 2 + yy // 2
        rows = pl.ds(pl.multiple_of(q * JT, JT), JT)
        part = nt(t[rows, :].astype(BF), bst[...])
        for h in range(2):
            gm[h, q] = part[:, 128 * h:128 * h + 128].reshape(4, 128, 128)
        if k:
            s1b.append(send(gm.at[1, q], rb.at[n], ys[n][1]))
        for i, (xx, to) in enumerate(xs):
            s1a.append(send(gm.at[0, q, xx], ra.at[i, q], to))

    rolled = pltpu.roll(perr[...], (S - LIVE * m) % S, 1)[:, 0:PAD]
    metav[0:2, :] = jnp.where(valid, rolled[0:2], 0.0)
    metav[2:4, :] = rowmeta[0:2, :]
    metav[4:8, :] = jnp.zeros((4, PAD), F32)
    stores = [pltpu.make_async_copy(metav, meta_out, lsem.at[18])]
    stores[0].start()
    square = rolled[2:3] * rolled[2:3] + rolled[3:4] * rolled[3:4]
    square = jnp.where(valid, square, 0.0)
    chosen = iota((DEVICES, PAD), 0).astype(F32) == rowmeta[2:3, :]
    loss_col = jnp.sum(jnp.where(chosen, square, 0.0), axis=1, keepdims=True)
    count_col = jnp.sum(jnp.where(chosen, 1.0, 0.0), axis=1, keepdims=True)
    loss_row = jnp.broadcast_to(loss_col, (DEVICES, DEVICES)).T[0:1]
    count_row = jnp.broadcast_to(count_col, (DEVICES, DEVICES)).T[0:1]

    def back(q, _):
        rows = pl.ds(pl.multiple_of(q * JT, JT), JT)
        wc = jnp.concatenate([w[0, q].reshape(JT, 128), w[1, q].reshape(JT, 128)], axis=1)
        acc = jnp.zeros((16, JT), F32)
        for s in range(NCH):
            sl = slice(CH * s, CH * s + CH)
            act = t[rows, sl]
            bf = (nn(wc, bst[:, sl]) * (1.0 - act * act)).astype(BF)
            acc = acc + nt(feats[:, sl], bf)
        gwp[:, rows] = acc
        return 0

    lax.fori_loop(0, H // JT - 1, back, 0)
    slab_loads = [
        pltpu.make_async_copy(flat_flow, t.at[0:1280, 0:512], lsem.at[11]),
        pltpu.make_async_copy(diff_h, t.at[0:256, 512:1024], lsem.at[12]),
    ]
    for copy in slab_loads:
        copy.start()
    back(H // JT - 1, 0)
    gwp[12:16, :] = jnp.zeros((4, H), F32)
    gwp[12:13, 0:DEVICES] = loss_row
    gwp[13:14, 0:DEVICES] = count_row

    def stencil(v):
        row, col = iota((32, 512), 0), iota((32, 512), 1)
        for l in range(8):
            at = v * 256 + l * 32
            u = t[at:at + 32, 0:512]
            low, high = halo[0, v, l:l + 1, :], halo[1, v, l:l + 1, :]
            below_z = jnp.where(row == 0, low, pltpu.roll(u, 1, 0))
            above_z = jnp.where(row == 31, high, pltpu.roll(u, 31, 0))
            below_x = jnp.where(col == 0, u, pltpu.roll(u, 1, 1))
            above_x = jnp.where(col == 511, u, pltpu.roll(u, 511, 1))
            below_y = t[at - 32:at, 0:512] if l > 0 else u
            above_y = t[at + 32:at + 64, 0:512] if l < 7 else u
            spread = below_x + above_x + below_y + above_y + below_z + above_z - 6.0 * u
            value = u + ADVECT * (below_x - u) + t[l * 32:l * 32 + 32, 512:1024] * spread
            t[at:at + 32, 1024:1536] = value
        rows = slice(v * 256, v * 256 + 256)
        copy = pltpu.make_async_copy(t.at[rows, 1024:1536], adv_out.at[rows, :], lsem.at[13 + v])
        copy.start()
        stores.append(copy)

    g1 = [
        send(gwp.at[:, pl.ds(pl.multiple_of(mm * COLS, COLS), COLS)], rg.at[i], to)
        for i, (mm, to) in enumerate(members)
    ]
    for copy in s1a + s1b + halos + slab_loads:
        copy.wait()
    gm[0, :, x] = gm[0, :, x] + ra[0] + ra[1] + ra[2]
    gm[1, yq] = gm[1, yq] + rb[0] + rb[1] + rb[2]
    s2 = [send(gm.at[0, yy, x], r2a.at[i], to) for i, (yy, to) in enumerate(ys)]
    s2 += [send(gm.at[1, yq, xx], r2b.at[i], to) for i, (xx, to) in enumerate(xs)]

    stencil(0)
    my_cols = pl.ds(pl.multiple_of(m * COLS, COLS), COLS)
    stencil(1)
    for copy in g1:
        copy.wait()
    part = gwp[:, my_cols]
    for i in range(7):
        part = part + rg[i]
    rgp[yq * 4 + x] = part
    g2 = [send(rgp.at[yq * 4 + x], rgp.at[yq * 4 + x], to) for to in plane]

    stencil(2)
    for copy in s2:
        copy.wait()
    fin[0] = gm[0, yq, x] + r2a[0] + r2a[1] + r2a[2]
    fin[1] = gm[1, yq, x] + r2b[0] + r2b[1] + r2b[2]
    s3 = [
        send(fin.at[:, pl.ds(pl.multiple_of(mm * 16, 16), 16), :], gmid_out.at[m], to)
        for mm, to in members
    ]
    stores.append(pltpu.make_async_copy(fin.at[:, mine, :], gmid_out.at[m], lsem.at[19]))
    stores[-1].start()
    stencil(3)

    for copy in g2:
        copy.wait()
    part = rgp[0]
    for i in range(1, 16):
        part = part + rgp[i]
    smallv[...] = part
    g4 = [send(smallv, small_out.at[m], to) for _, to in members]
    stores.append(pltpu.make_async_copy(smallv, small_out.at[m], lsem.at[20]))
    stores[-1].start()
    stencil(4)
    for copy in s3 + g4 + stores:
        copy.wait()


N_SENDS = 7 + 7 + 6 + 18 + 2 + 28 + 12 + 3 + 6 + 7 + 7 + 15 + 7


def train(flow, diff, counts, routes, index, win, wmid, wout):
    sds = jax.ShapeDtypeStruct
    return pl.pallas_call(
        train_kernel,
        out_shape=(
            sds((1280, 512), F32),
            sds((8, PAD), F32),
            sds((GROUP, 16, COLS), F32),
            sds((GROUP, 2, 16, 128), F32),
        ),
        in_specs=[pl.BlockSpec(memory_space=pl.ANY)] * 9,
        out_specs=(pl.BlockSpec(memory_space=pl.ANY),) * 4,
        scratch_shapes=[
            pltpu.VMEM((H, S), F32),
            pltpu.VMEM((H, 1920), BF),
            pltpu.VMEM((2, 4, 4, 128, 128), BF),
            pltpu.VMEM((COLS, H), BF),
            pltpu.VMEM((COLS, S), F32),
            pltpu.VMEM((COLS, S), BF),
            pltpu.VMEM((2, 4, 4, 128, 128), F32),
            pltpu.VMEM((3, 4, 128, 128), F32),
            pltpu.VMEM((3, 4, 128, 128), F32),
            pltpu.VMEM((3, 128, 128), F32),
            pltpu.VMEM((3, 128, 128), F32),
            pltpu.VMEM((2, 128, 128), F32),
            pltpu.VMEM((4, 3, 32, 512), F32),
            pltpu.VMEM((2, 2, 32, 512), F32),
            pltpu.VMEM((2, 5, 8, 512), F32),
            pltpu.VMEM((GROUP, 2, 16, 128), BF),
            pltpu.VMEM((H, 16), BF),
            pltpu.VMEM((16, COLS), F32),
            pltpu.VMEM((2, 5, 8, 512), F32),
            pltpu.VMEM((GROUP, 16, PAD), BF),
            pltpu.VMEM((16, S + 128), F32),
            pltpu.VMEM((16, S), BF),
            pltpu.VMEM((GROUP, len(PARTS), 2, CH), F32),
            pltpu.VMEM((8, PAD), F32),
            pltpu.VMEM((8, S), F32),
            pltpu.VMEM((16, H), F32),
            pltpu.VMEM((7, 16, COLS), F32),
            pltpu.VMEM((16, 16, COLS), F32),
            pltpu.VMEM((1, TILES), jnp.int32),
            pltpu.VMEM((1, TILES), jnp.int32),
            pltpu.VMEM((CAP, TILES), jnp.int32),
            pltpu.VMEM((12, H), BF),
            pltpu.VMEM((16, H), BF),
            pltpu.VMEM((2, H), BF),
            pltpu.VMEM((16, TILES), F32),
            pltpu.VMEM((8, PAD), F32),
            pltpu.VMEM((16, COLS), F32),
            pltpu.SemaphoreType.DMA((21,)),
            pltpu.SemaphoreType.DMA((N_SENDS,)),
            pltpu.SemaphoreType.DMA((N_SENDS,)),
        ],
        compiler_params=pltpu.CompilerParams(
            collective_id=0, has_side_effects=True, vmem_limit_bytes=62 * 2**20
        ),
        name="train",
    )(flow, flow.reshape(1280, 512), diff.reshape(256, 512), counts, routes.reshape(1, TILES), index.T, win, wmid, wout)


def finish_kernel(
    adv, stress_h, meta_h, small_h, gmid_h, field, new_stress, loss, gw, gwm,
    held, stress, meta, small, gmid, wall, gwv, gwmv, sem,
):
    order = (1, 3, 0, 2, 4)
    first = [
        pltpu.make_async_copy(meta_h, meta, sem.at[10]),
        pltpu.make_async_copy(stress_h, stress, sem.at[11]),
    ]
    then = [
        pltpu.make_async_copy(small_h, small, sem.at[12]),
        pltpu.make_async_copy(gmid_h, gmid, sem.at[13]),
    ]
    loads = {v: pltpu.make_async_copy(adv.at[v], held.at[v], sem.at[v]) for v in order}
    stores = {v: pltpu.make_async_copy(held.at[v], field.at[v], sem.at[5 + v]) for v in order}
    last = [
        pltpu.make_async_copy(wall, new_stress, sem.at[14]),
        pltpu.make_async_copy(gwv, gw, sem.at[15]),
        pltpu.make_async_copy(gwmv, gwm, sem.at[16]),
    ]
    for copy in first + [loads[v] for v in order] + then:
        copy.start()
    first[0].wait()
    zrow, xrow = meta[2:3, :], meta[3:4, :]
    oz = jnp.where(iota((32, PAD), 0).astype(F32) == zrow, 1.0, 0.0)
    ox = jnp.where(iota((PAD, PAD), 0).astype(F32) == xrow, 1.0, 0.0).astype(BF)
    lhs = jnp.concatenate([oz * meta[0:1, :], oz * meta[1:2, :], oz], axis=0).astype(BF)
    spread = nt(lhs, ox)
    hit = spread[64:96] > 0.5
    first[1].wait()
    for v in (0, 2, 4):
        loads[v].wait()
        stores[v].start()
    for i, v in enumerate((1, 3)):
        value = jnp.where(hit, spread[32 * i:32 * i + 32], stress[i])
        wall[i] = value
        loads[v].wait()
        held[v, 0] = held[v, 0] - GAIN * value
        stores[v].start()
    last[0].start()
    for copy in then:
        copy.wait()
    for i in range(GROUP):
        gwv[:, COLS * i:COLS * i + COLS] = small[i, 0:12, :]
        for h in range(2):
            at = COLS * i + 128 * h
            gwmv[:, at:at + 128] = gmid[i, h]
    last[1].start()
    last[2].start()
    me = lax.axis_index("sec") * 64 + lax.axis_index("dev")
    ratio = 0.5 * small[0, 12:13, 0:DEVICES] / small[0, 13:14, 0:DEVICES]
    loss[0] = jnp.sum(jnp.where(iota((1, DEVICES), 1) == me, ratio, 0.0))
    for copy in [stores[v] for v in order] + last:
        copy.wait()


def finish(adv, stress, meta, small, gmid):
    sds = jax.ShapeDtypeStruct
    anywhere = pl.BlockSpec(memory_space=pl.ANY)
    return pl.pallas_call(
        finish_kernel,
        out_shape=(
            sds((5, 8, 32, 512), F32),
            sds((2, 32, 512), F32),
            sds((1,), F32),
            sds((12, H), F32),
            sds((16, H), F32),
        ),
        in_specs=[anywhere] * 5,
        out_specs=(anywhere, anywhere, pl.BlockSpec(memory_space=pltpu.SMEM), anywhere, anywhere),
        scratch_shapes=[
            pltpu.VMEM((5, 8, 32, 512), F32),
            pltpu.VMEM((2, 32, 512), F32),
            pltpu.VMEM((8, PAD), F32),
            pltpu.VMEM((GROUP, 16, COLS), F32),
            pltpu.VMEM((GROUP, 2, 16, 128), F32),
            pltpu.VMEM((2, 32, 512), F32),
            pltpu.VMEM((12, H), F32),
            pltpu.VMEM((16, H), F32),
            pltpu.SemaphoreType.DMA((17,)),
        ],
        compiler_params=pltpu.CompilerParams(vmem_limit_bytes=62 * 2**20),
        name="finish",
    )(adv.reshape(5, 8, 32, 512), stress, meta, small, gmid)


def body(flow, diff, stress, counts, routes, index, win, wmid, wout):
    adv, meta, small, gmid = train(flow, diff, counts, routes, index, win, wmid, wout)
    return finish(adv, stress, meta, small, gmid)


def solution(mesh):
    both = ("sec", "dev")
    in_specs = (
        P(None, None, both, None), P(None, both, None), P(None, both, None),
        P(both, None), P(both, None), P(both, None), P(), P(both, None), P(),
    )
    out_specs = (P(None, None, both, None), P(None, both, None), P(both), P(), P(both, None))
    return jax.shard_map(body, mesh=mesh, in_specs=in_specs, out_specs=out_specs, check_vma=False)
```
